256 devices in a mesh: kv: 32 (over z, y), tp: 8 (over x, core).
Axes of the slice: x: 4, y: 4, z: 8, core: 2. Of those that a mesh axis runs over, the one named last changes fastest.
Arguments:
- q_nope: bfloat16 [16, 16384], P(None, 'tp'), may hold values from -6 to 6
- q_rope: bfloat16 [16, 8192], P(None, 'tp'), may hold values from -4 to 4
- w_absorb: bfloat16 [128, 128, 512], P('tp'), may hold values from -0.5 to 0.5
- w_value: bfloat16 [128, 512, 128], P('tp'), may hold values from -0.25 to 0.25
- w_out: bfloat16 [16384, 7168], P('tp', 'kv'), may hold values from -0.046875 to 0.046875
- kv_cache: bfloat16 [256, 256, 576], P('kv'), may hold values from -40 to 40
- new_latent: bfloat16 [16, 576], replicated, may hold values from -8 to 8
- lengths: int32 [16], replicated, may hold values from 1 to 4096, as said below
- page_table: int32 [16, 16], replicated, may hold values from -1 to 255, as said below
- residual: bfloat16 [16, 7168], P(None, 'kv'), may hold values from -5 to 5
- norm_gain: bfloat16 [7168], P('kv'), may hold values from 0.5 to 1.5
- w_gate: bfloat16 [7168, 18432], P('kv', 'tp'), may hold values from -0.0625 to 0.0625
- w_up: bfloat16 [7168, 18432], P('kv', 'tp'), may hold values from -0.0625 to 0.0625
- w_down: bfloat16 [18432, 7168], P('tp', 'kv'), may hold values from -0.046875 to 0.046875
Outputs:
- output: bfloat16 [16, 7168], P(None, 'kv')
The draws below stay inside these ranges and needn't reach their ends.
Inputs may be any that keep to these rules, and one draw needn't show every extreme that they name: `lengths`: cached tokens of each request; the longest has exactly 4096. page_table[r, j] is the slot (index along the first dimension of kv_cache) that holds tokens j * 256 to j * 256 + 255 of request r for j below ceil(lengths[r] / 256), and -1 for the other j; no slot is named twice. Slots that no entry names hold no data that is read.
All inputs are finite; a program needn't handle non-finite values.
Results may differ from the reference program's by a relative error of at most 0.014.
Values may be sent and summed in bfloat16 or wider, within the bound.
No kernel may reach another device: no remote copies, remote signals or barrier semaphores. Data moves between devices by JAX's collectives and lax.ppermute only.
A program may use at most 128 MiB of HBM per device.

```python
import math
import jax
import jax.numpy as jnp
from jax import lax

D = 7168
FF = 18432
HEADS = 128
LAT = 512
ROPE = 64
NOPE = 128
VHEAD = 128
PAGE = 256
REQS = 16
PAGES_DEV = 8
CTX = 576
SLOTS = 256
MAX_PAGES = 16
N_KV = 32


def page_layout(key):
    counts = jax.random.randint(jax.random.fold_in(key, 11), (REQS,), 1, MAX_PAGES + 1)
    longest = jax.random.randint(jax.random.fold_in(key, 12), (), 0, REQS)
    request_ids = jnp.arange(REQS, dtype=jnp.int32)
    counts = jnp.where(request_ids == longest, MAX_PAGES, counts).astype(jnp.int32)
    tail_tokens = jax.random.randint(jax.random.fold_in(key, 13), (REQS,), 1, PAGE + 1)
    lengths_out = jnp.where(request_ids == longest, MAX_PAGES * PAGE, (counts - 1) * PAGE + tail_tokens).astype(jnp.int32)
    starts = (jnp.cumsum(counts) - counts).astype(jnp.int32)
    device_order = jax.random.permutation(jax.random.fold_in(key, 14), N_KV).astype(jnp.int32)
    slot_order = jax.random.permutation(jax.random.fold_in(key, 15), PAGES_DEV).astype(jnp.int32)
    ranks = jnp.arange(SLOTS, dtype=jnp.int32)
    slot_of_rank = device_order[ranks // PAGES_DEV] * PAGES_DEV + slot_order[ranks % PAGES_DEV]
    page_ids = jnp.arange(MAX_PAGES, dtype=jnp.int32)
    linear = jnp.minimum(starts[:, None] + page_ids[None, :], SLOTS - 1)
    page_slots = jnp.where(page_ids[None, :] < counts[:, None], slot_of_rank[linear], -1).astype(jnp.int32)
    return (lengths_out, page_slots)


def draw_lengths(key, part):
    return page_layout(key)[0]


def draw_page_table(key, part):
    return page_layout(key)[1]


def draw_kv_cache(key, part):
    key = jax.random.fold_in(key, 3)
    entries = jnp.clip(jax.random.normal(key, (SLOTS, PAGE, CTX), jnp.float32), -6.0, 6.0)
    return entries.astype(jnp.bfloat16)


def draw_q_rope(key, part):
    key = jax.random.fold_in(key, 5)
    noise = jnp.clip(jax.random.normal(key, (REQS, HEADS, ROPE), jnp.float32), -4.0, 4.0)
    return noise.reshape(REQS, HEADS * ROPE).astype(jnp.bfloat16)


def rising(column, factor):
    return jnp.exp(math.log(factor) * column)


def draw_residual(key, part):
    key = jax.random.fold_in(key, 9)
    base = jnp.clip(jax.random.normal(key, (REQS, D), jnp.float32), -6.0, 6.0)
    column = jnp.arange(D, dtype=jnp.float32) / D
    spread = jnp.exp(jax.random.uniform(jax.random.fold_in(key, 1), (D,), jnp.float32, 0.0, math.log(10.0)))
    scaled = 0.02 * base * spread * rising(column, 10.0)
    return jnp.clip(scaled, -5.0, 5.0).astype(jnp.bfloat16)


def level_of(stream_key, dims, shards, low, top_value):
    loudness = 1.0
    for position, blocks in shards:
        draws = jax.random.uniform(jax.random.fold_in(jax.random.fold_in(stream_key, 6), position), (blocks,), jnp.float32, low / len(shards), top_value / len(shards))
        loudness = loudness * jnp.repeat(jnp.exp(draws), dims[position] // blocks).reshape((-1,) + (1,) * (len(dims) - 1 - position))
    return loudness


def gaussian(stream_key, shape, width, most, split=(), kind=jnp.bfloat16):
    result = width * jax.random.normal(stream_key, shape, jnp.float32)
    if split:
        result = result * level_of(stream_key, shape, split, -0.22, 0.18)
    return jnp.clip(result, -most, most).astype(kind)


def setup_inputs(seed: int = 0) -> dict:
    arg_keys = jax.random.split(jax.random.key(seed), 15)
    return {
        "q_nope": gaussian(arg_keys[0], (REQS, HEADS * NOPE), 1.0, 6.0, ((1, 8),)),
        "q_rope": draw_q_rope(jax.random.fold_in(arg_keys[14], 71), 0),
        "w_absorb": gaussian(arg_keys[2], (HEADS, NOPE, LAT), NOPE ** -0.5, 0.5, ((0, 8),)),
        "w_value": gaussian(arg_keys[3], (HEADS, LAT, VHEAD), LAT ** -0.5, 0.25, ((0, 8),)),
        "w_out": gaussian(arg_keys[4], (HEADS * VHEAD, D), (HEADS * VHEAD) ** -0.5, 0.046875, ((0, 8), (1, 32))),
        "kv_cache": draw_kv_cache(jax.random.fold_in(arg_keys[14], 71), 0),
        "new_latent": gaussian(arg_keys[6], (REQS, CTX), 2.0, 8.0),
        "lengths": draw_lengths(jax.random.fold_in(arg_keys[14], 71), 0),
        "page_table": draw_page_table(jax.random.fold_in(arg_keys[14], 71), 0),
        "residual": draw_residual(jax.random.fold_in(arg_keys[14], 71), 0),
        "norm_gain": jnp.clip(1.0 + 0.1 * jax.random.normal(arg_keys[10], (D,), jnp.float32), 0.5, 1.5).astype(jnp.bfloat16),
        "w_gate": gaussian(arg_keys[11], (D, FF), D ** -0.5, 0.0625, ((0, 32), (1, 8))),
        "w_up": gaussian(arg_keys[12], (D, FF), D ** -0.5, 0.0625, ((0, 32), (1, 8))),
        "w_down": gaussian(arg_keys[13], (FF, D), FF ** -0.5, 0.046875, ((0, 8), (1, 32))),
    }


def reference(q_nope, q_rope, w_absorb, w_value, w_out, kv_cache, new_latent, lengths, page_table, residual, norm_gain, w_gate, w_up, w_down):
    f32 = jnp.float32
    requests = q_nope.shape[0]
    score_scale = 1.0 / jnp.sqrt(f32(NOPE + ROPE))
    q_lat = jnp.einsum('rhn,hnl->rhl', q_nope.reshape(requests, HEADS, NOPE).astype(f32), w_absorb.astype(f32)).astype(jnp.bfloat16)
    queries = jnp.concatenate([q_lat, q_rope.reshape(requests, HEADS, ROPE)], axis=-1)
    slot_ids = jnp.arange(SLOTS, dtype=jnp.int32)
    matches = page_table[:, :, None] == slot_ids[None, None, :]
    slot_live = jnp.any(matches, axis=(0, 1))
    slot_req = lax.optimization_barrier(jnp.sum(jnp.where(matches, jnp.arange(requests, dtype=jnp.int32)[:, None, None], 0), axis=(0, 1))).astype(jnp.int32)
    slot_page = lax.optimization_barrier(jnp.sum(jnp.where(matches, jnp.arange(MAX_PAGES, dtype=jnp.int32)[None, :, None], 0), axis=(0, 1))).astype(jnp.int32)
    picked = jnp.take(queries, slot_req, axis=0)
    scores = jnp.einsum('shc,stc->sht', picked.astype(f32), kv_cache.astype(f32)) * score_scale
    token_pos = slot_page[:, None] * PAGE + jnp.arange(PAGE, dtype=jnp.int32)[None, :]
    is_live = slot_live[:, None] & (token_pos < jnp.take(lengths, slot_req)[:, None])
    live3 = is_live[:, None, :]
    page_max = lax.optimization_barrier(jnp.max(jnp.where(live3, scores, f32(-1e+30)), axis=-1))
    weights = jnp.where(live3, jnp.exp(scores - page_max[..., None]), f32(0.0)).astype(jnp.bfloat16)
    page_sum = lax.optimization_barrier(jnp.sum(weights.astype(f32), axis=-1))
    page_acc = jnp.einsum('sht,stl->shl', weights.astype(f32), kv_cache[:, :, :LAT].astype(f32))
    owners = (slot_req[:, None] == jnp.arange(requests, dtype=jnp.int32)[None, :]) & slot_live[:, None]
    owners3 = owners[:, :, None]
    cache_max = lax.optimization_barrier(jnp.max(jnp.where(owners3, page_max[:, None, :], f32(-1e+30)), axis=0))
    factor = jnp.exp(jnp.where(owners3, page_max[:, None, :] - cache_max[None], f32(-1e+30)))
    cache_sum = jnp.einsum('srh,sh->rh', factor, page_sum, precision=lax.Precision.HIGHEST)
    cache_acc = jnp.einsum('srh,shl->rhl', factor, page_acc, precision=lax.Precision.HIGHEST)
    new_score = jnp.einsum('rhc,rc->rh', queries.astype(f32), new_latent.astype(f32)) * score_scale
    highest = jnp.maximum(cache_max, new_score)
    keep_old = jnp.exp(cache_max - highest)
    keep_new = jnp.exp(new_score - highest)
    numer = cache_acc * keep_old[..., None] + keep_new[..., None] * new_latent[:, None, :LAT].astype(f32)
    o_lat = numer / (cache_sum * keep_old + keep_new)[..., None]
    o_value = jnp.einsum('rhl,hlv->rhv', o_lat, w_value.astype(f32), precision=lax.Precision.HIGHEST).astype(jnp.bfloat16).reshape(requests, HEADS * VHEAD)
    hidden = residual.astype(f32) + jnp.dot(o_value, w_out, preferred_element_type=f32)
    squares = lax.optimization_barrier(jnp.mean(hidden * hidden, axis=-1, keepdims=True))
    normed = (hidden * lax.rsqrt(squares + 1e-06) * norm_gain.astype(f32)).astype(jnp.bfloat16)
    gate_sum = jnp.dot(normed, w_gate, preferred_element_type=f32)
    up_sum = jnp.dot(normed, w_up, preferred_element_type=f32)
    activation = (jax.nn.silu(gate_sum) * up_sum).astype(jnp.bfloat16)
    return (hidden + jnp.dot(activation, w_down, preferred_element_type=f32)).astype(jnp.bfloat16)
```

```python
import math

import jax
import jax.numpy as jnp
from jax import lax
from jax.sharding import PartitionSpec as P

D = 7168
LOW = -1e30


def exchange(x, axis):
    return lax.all_to_all(x, axis, 0, 0)


def spread(x, axis):
    copies = jnp.broadcast_to(x[None], (lax.axis_size(axis),) + x.shape)
    return exchange(copies, axis)


def on_device(
    q_nope,
    q_rope,
    w_absorb,
    w_value,
    w_out,
    kv_cache,
    new_latent,
    lengths,
    page_table,
    residual,
    norm_gain,
    w_gate,
    w_up,
    w_down,
):
    f32 = jnp.float32
    bf16 = jnp.bfloat16
    requests = q_nope.shape[0]
    heads_here, nope_width, latent = w_absorb.shape
    rope_width = q_rope.shape[1] // heads_here
    slots_here, page_len, _ = kv_cache.shape
    max_pages = page_table.shape[1]
    value_width = w_value.shape[2]
    n_kv = lax.axis_size("kv")
    slots = n_kv * slots_here
    per_head = n_kv // heads_here
    part = value_width // per_head
    me = lax.axis_index("kv")
    score_scale = 1.0 / math.sqrt(nope_width + rope_width)

    matches = page_table[:, :, None] == jnp.arange(slots, dtype=jnp.int32)[None, None, :]
    owns = jnp.any(matches, axis=1)
    slot_live = jnp.any(owns, axis=0)
    slot_req = jnp.sum(jnp.where(owns, jnp.arange(requests, dtype=jnp.int32)[:, None], 0), axis=0)
    slot_page = jnp.sum(
        jnp.where(matches, jnp.arange(max_pages, dtype=jnp.int32)[None, :, None], 0), axis=(0, 1)
    )
    slot_tokens = jnp.sum(jnp.where(owns, lengths[:, None], 0), axis=0) - slot_page * page_len

    def mine(x):
        return lax.dynamic_slice_in_dim(x, me * slots_here, slots_here)

    my_req = mine(slot_req)
    my_tokens = mine(jnp.where(slot_live, slot_tokens, 0))

    q_lat = jnp.einsum(
        "rhn,hnl->rhl",
        q_nope.reshape(requests, heads_here, nope_width),
        w_absorb,
        preferred_element_type=f32,
    ).astype(bf16)
    queries = jnp.concatenate([q_lat, q_rope.reshape(requests, heads_here, rope_width)], axis=-1)
    picked = jnp.take(queries, my_req, axis=0)
    scores = jnp.einsum("shc,stc->sht", picked, kv_cache, preferred_element_type=f32) * score_scale
    is_live = jnp.arange(page_len, dtype=jnp.int32)[None, :] < my_tokens[:, None]
    live3 = is_live[:, None, :]
    page_max = jnp.max(jnp.where(live3, scores, f32(LOW)), axis=-1)
    weights = jnp.where(live3, jnp.exp(scores - page_max[..., None]), f32(0.0)).astype(bf16)
    page_sum = jnp.sum(weights.astype(f32), axis=-1)
    page_acc = jnp.einsum(
        "sht,stl->shl", weights, kv_cache[:, :, :latent], preferred_element_type=f32
    )
    acc_high = page_acc.astype(bf16)
    acc_low = (page_acc - acc_high.astype(f32)).astype(bf16)
    new_lat = jnp.broadcast_to(new_latent[:, None, :latent], (requests, heads_here, latent))
    rows = jnp.concatenate([acc_high, acc_low, new_lat], axis=0)
    valued = jnp.einsum("xhl,hlv->hxv", rows, w_value, preferred_element_type=f32)
    page_value = valued[:, :slots_here] + valued[:, slots_here : 2 * slots_here]
    new_value = valued[:, 2 * slots_here :]
    new_score = (
        jnp.einsum("rhc,rc->hr", queries, new_latent, preferred_element_type=f32) * score_scale
    )

    page_value = page_value.reshape(heads_here, slots_here, per_head, part).transpose(0, 2, 1, 3)
    stats = jnp.stack([page_max.T, page_sum.T], axis=-1)[:, None]
    stats = jnp.broadcast_to(stats, (heads_here, per_head, slots_here, 2))
    stats = jnp.pad(stats, ((0, 0), (0, 0), (0, 0), (0, 128 - 2 - part)))
    payload = jnp.concatenate([page_value, stats], axis=-1).reshape(n_kv, slots_here, 128)
    pages = exchange(payload, "kv").reshape(slots, 128)
    my_head = me // per_head
    my_new_score = lax.dynamic_index_in_dim(new_score, my_head, 0, False)
    my_new_value = lax.dynamic_index_in_dim(new_value, my_head, 0, False)
    my_new_value = lax.dynamic_slice_in_dim(my_new_value, (me % per_head) * part, part, axis=1)
    slot_max = jnp.where(owns, pages[:, part][None, :], f32(LOW))
    top = jnp.maximum(jnp.max(slot_max, axis=1), my_new_score)
    factor = jnp.where(owns, jnp.exp(slot_max - top[:, None]), f32(0.0))
    keep_new = jnp.exp(my_new_score - top)
    total = jnp.sum(factor * pages[:, part + 1][None, :], axis=1) + keep_new
    value = jnp.dot(factor, pages[:, :part], precision=lax.Precision.HIGHEST)
    my_value = ((value + keep_new[:, None] * my_new_value) / total[:, None]).astype(bf16)

    o_value = spread(my_value, "kv").transpose(1, 0, 2).reshape(requests, n_kv * part)
    attention = jnp.sum(spread(jnp.dot(o_value, w_out, preferred_element_type=f32), "tp"), axis=0)
    hidden = residual.astype(f32) + attention

    squares = jnp.sum(hidden * hidden, axis=-1)
    gained = (hidden * norm_gain.astype(f32)).astype(bf16)
    gate_part = jnp.dot(gained, w_gate, preferred_element_type=f32)
    up_part = jnp.dot(gained, w_up, preferred_element_type=f32)
    units = w_gate.shape[1] // n_kv

    def cut(x):
        return x.astype(bf16).reshape(requests, n_kv, units).transpose(1, 0, 2)

    sq_high = squares.astype(bf16)
    sq_low = (squares - sq_high.astype(f32)).astype(bf16)
    sq = jnp.broadcast_to(jnp.stack([sq_high, sq_low], axis=-1)[None], (n_kv, requests, 2))
    sums = exchange(jnp.concatenate([cut(gate_part), cut(up_part), sq], axis=-1), "kv")
    sums = jnp.sum(sums.astype(f32), axis=0)
    scale = lax.rsqrt((sums[:, 2 * units] + sums[:, 2 * units + 1]) / D + 1e-06)[:, None]
    gate_sum = sums[:, :units] * scale
    up_sum = sums[:, units : 2 * units] * scale
    my_activation = (jax.nn.silu(gate_sum) * up_sum).astype(bf16)
    activation = spread(my_activation, "kv").transpose(1, 0, 2).reshape(requests, n_kv * units)
    down_part = jnp.dot(activation, w_down, preferred_element_type=f32)
    projected = jnp.sum(spread(down_part, "tp"), axis=0)
    return (hidden + projected).astype(bf16)


def solution(mesh):
    return jax.shard_map(
        on_device,
        mesh=mesh,
        in_specs=(
            P(None, "tp"),
            P(None, "tp"),
            P("tp", None, None),
            P("tp", None, None),
            P("tp", "kv"),
            P("kv", None, None),
            P(),
            P(),
            P(),
            P(None, "kv"),
            P("kv"),
            P("kv", "tp"),
            P("kv", "tp"),
            P("tp", "kv"),
        ),
        out_specs=P(None, "kv"),
        check_vma=False,
    )
```

```python
import functools
import math

import jax
import jax.numpy as jnp
from jax import lax
from jax.experimental import pallas as pl
from jax.experimental.pallas import tpu as pltpu
from jax.sharding import PartitionSpec as P

D = 7168
LOW = -1e30
LANES = 128
HALF = LANES // 2
F32 = jnp.float32
BF16 = jnp.bfloat16
HIGHEST = lax.Precision.HIGHEST
VMEM = pl.BlockSpec(memory_space=pltpu.VMEM)
SMEM = pl.BlockSpec(memory_space=pltpu.SMEM)
HBM = pl.BlockSpec(memory_space=pltpu.HBM)


def dot(a, b, precision=None):
    return jnp.dot(a, b, preferred_element_type=F32, precision=precision)


def dot_nt(a, b):
    return lax.dot_general(a, b, (((1,), (1,)), ((), ())), preferred_element_type=F32)


def dot_tn(a, b):
    return lax.dot_general(a, b, (((0,), (0,)), ((), ())), preferred_element_type=F32)


def iota(shape, dim):
    return lax.broadcasted_iota(jnp.int32, shape, dim)


def swap_halves_if(flag, x):
    return jnp.where(flag == 1, pltpu.roll(x, HALF, 1), x)


def attend(
    scale,
    me_ref,
    lengths_hbm,
    table_hbm,
    q_nope_hbm,
    q_rope_hbm,
    absorb_hbm,
    pages_hbm,
    value_hbm,
    new_hbm,
    out_ref,
    new_out_ref,
    lengths_ref,
    table_ref,
    q_nope_ref,
    q_rope_ref,
    absorb_ref,
    pages_ref,
    value_ref,
    new_ref,
    q_scr,
    acc_scr,
    sems,
    page_sems,
):
    heads, nope, latent = absorb_ref.shape
    slots, ctx, page_len = pages_ref.shape
    rope = ctx - latent
    requests = new_ref.shape[0]
    me = me_ref[0]
    lane = iota((slots, LANES), 1)
    blocks = latent // LANES

    def fetch(source, target, sem):
        copy = pltpu.make_async_copy(source, target, sem)
        copy.start()
        return copy

    lengths_in = fetch(lengths_hbm, lengths_ref, sems.at[0])
    table_in = fetch(table_hbm, table_ref, sems.at[1])
    q_nope_in = fetch(q_nope_hbm, q_nope_ref, sems.at[2])
    q_rope_in = fetch(q_rope_hbm, q_rope_ref, sems.at[3])
    absorb_in = fetch(absorb_hbm, absorb_ref, sems.at[4])
    pages_in = [
        fetch(pages_hbm.at[s], pages_ref.at[s], page_sems.at[s]) for s in range(slots)
    ]
    value_in = fetch(value_hbm, value_ref, sems.at[5])
    new_in = fetch(new_hbm, new_ref, sems.at[6])

    lengths_in.wait()
    table_in.wait()
    table = table_ref[...]
    row = iota(table.shape, 0)
    left = iota(table.shape, 1) * -page_len
    for r in range(requests):
        left = left + jnp.where(row == r, lengths_ref[r], 0)
    left = left.astype(F32)
    owner = jnp.zeros((requests, slots), F32)
    tokens = []
    for s in range(slots):
        match = table == me * slots + s
        column = jnp.max(jnp.where(match, 1.0, 0.0), axis=1, keepdims=True)
        owner = owner + jnp.where(iota(owner.shape, 1) == s, column, 0.0)
        found = jnp.sum(jnp.where(match, left, 0.0), axis=1, keepdims=True)
        tokens.append(jnp.sum(found, axis=0, keepdims=True).astype(jnp.int32))
    owner = owner.astype(BF16)

    q_nope_in.wait()
    q_rope_in.wait()
    picked = dot_tn(owner, q_nope_ref[...]).astype(BF16)
    picked_rope = dot_tn(owner, q_rope_ref[...])
    absorb_in.wait()
    for h in range(heads):
        q_lat = dot(picked[:, h * nope : (h + 1) * nope], absorb_ref[h])
        rows = slice(h * slots, (h + 1) * slots)
        q_lat = q_lat.astype(BF16).astype(F32)
        for c in range(blocks):
            q_scr[c, rows] = q_lat[:, c * LANES : (c + 1) * LANES]
        q_scr[blocks, rows, :rope] = picked_rope[:, h * rope : (h + 1) * rope]

    for s in range(slots):
        pages_in[s].wait()
        every = pl.ds(s, heads, stride=slots)
        q_low = [q_scr[c, every, :] for c in range(blocks)]
        q_low = jnp.concatenate(q_low, axis=1).astype(BF16)
        q_high = q_scr[blocks, every, :][:, :rope].astype(BF16)
        scores = dot(q_low, pages_ref[s, :latent, :]) + dot(q_high, pages_ref[s, latent:, :])
        live = iota(scores.shape, 1) < tokens[s]
        scores = jnp.where(live, scores * scale, LOW)
        most = jnp.max(scores, axis=1, keepdims=True)
        weights = jnp.where(live, jnp.exp(scores - most), 0.0).astype(BF16)
        total = jnp.sum(weights.astype(F32), axis=1, keepdims=True)
        rows = slice(s * heads, (s + 1) * heads)
        acc = dot_nt(weights, pages_ref[s, :latent, :])
        for c in range(blocks):
            acc_scr[c, rows] = acc[:, c * LANES : (c + 1) * LANES]
        stat_lane = iota((heads, LANES), 1)
        acc_scr[blocks, rows] = jnp.where(stat_lane < HALF + HALF // 2, most, total)

    value_in.wait()
    for h in range(heads):
        every = pl.ds(h, slots, stride=heads)
        acc = jnp.concatenate([acc_scr[c, every, :] for c in range(blocks)], axis=1)
        high = acc.astype(BF16).astype(F32)
        both = jnp.concatenate([high, acc - high], axis=0).astype(BF16)
        valued = dot(both, value_ref[h])
        valued = valued[:slots] + valued[slots:]
        stats = acc_scr[blocks, every, :]
        out_ref[2 * h] = jnp.where(lane < HALF, valued, stats)
        out_ref[2 * h + 1] = jnp.where(lane < HALF, pltpu.roll(valued, HALF, 1), stats)

    new_in.wait()
    head = me // 2
    fresh = new_ref[...]
    q_here = q_nope_ref[:, pl.ds(pl.multiple_of(head * nope, nope), nope)]
    q_lat = dot(q_here, absorb_ref[head]).astype(BF16).astype(F32)
    q_rot = q_rope_ref[:, pl.ds(pl.multiple_of((head // 2) * LANES, LANES), LANES)].astype(F32)
    q_rot = swap_halves_if(head % 2, q_rot)[:, :rope]
    fresh32 = fresh.astype(F32)
    score = jnp.sum(q_lat * fresh32[:, :latent], axis=1, keepdims=True)
    score = (score + jnp.sum(q_rot * fresh32[:, latent:], axis=1, keepdims=True)) * scale
    valued = swap_halves_if(me % 2, dot(fresh[:, :latent], value_ref[head]))
    lane = iota(valued.shape, 1)
    stats = jnp.where(lane < HALF + HALF // 2, score, 1.0)
    new_out_ref[...] = jnp.where(lane < HALF, valued, stats)


def combine(me_ref, table_ref, pages_ref, new_ref, out_ref):
    slots = pages_ref.shape[0]
    copies, requests, _ = out_ref.shape
    table = table_ref[...]
    slot = iota((requests, slots), 1)
    owns = slot < 0
    for j in range(table.shape[1]):
        owns = owns | (table[:, j : j + 1] == slot)
    pages = pages_ref[...]
    most = jnp.transpose(pages)[HALF : HALF + 1, :]
    most = jnp.where(owns, most, LOW)
    new = new_ref[...]
    new_score = new[:, HALF : HALF + 1]
    top = jnp.maximum(jnp.max(most, axis=1, keepdims=True), new_score)
    factor = jnp.where(owns, jnp.exp(most - top), 0.0)
    sums = dot(factor, pages, HIGHEST) + jnp.exp(new_score - top) * new
    value = sums / sums[:, LANES - 1 :]
    lane = iota(value.shape, 1)
    value = swap_halves_if(me_ref[0] % 2, jnp.where(lane < HALF, value, 0.0)).astype(BF16)
    for k in range(copies):
        out_ref[k] = value


def attention_out(parts_ref, weight_ref, out_ref):
    pairs = [parts_ref[2 * h] + parts_ref[2 * h + 1] for h in range(parts_ref.shape[0] // 2)]
    result = dot_nt(jnp.concatenate(pairs, axis=1), weight_ref[...])
    for t in range(out_ref.shape[0]):
        out_ref[t] = result


def gate_up(
    parts_ref, residual_ref, gain_ref, gate_ref, up_ref, out_ref, hidden_ref, gate_scr, up_scr, sq_scr
):
    requests = residual_ref.shape[0]
    copies = out_ref.shape[0]
    blocks = gate_ref.shape[1] // LANES
    share = blocks * requests // copies
    hidden = residual_ref[...].astype(F32)
    for t in range(parts_ref.shape[0]):
        hidden = hidden + parts_ref[t]
    hidden_ref[...] = hidden
    squares = jnp.sum(hidden * hidden, axis=1, keepdims=True)
    squares = jnp.broadcast_to(squares, (requests, LANES))
    for i in range(3):
        sq_scr[i * requests : (i + 1) * requests] = squares
    gained = (hidden * gain_ref[...].astype(F32)[None, :]).astype(BF16)
    for weight_ref, scr in ((gate_ref, gate_scr), (up_ref, up_scr)):
        part = dot(gained, weight_ref[...])
        for c in range(blocks):
            scr[c * requests : (c + 1) * requests] = part[:, c * LANES : (c + 1) * LANES]
    mine = iota((requests, LANES), 0) < share
    for k in range(copies):
        for i, scr in enumerate((gate_scr, up_scr)):
            start = (k * share - share + i * (requests - share)) % requests
            own = scr[k * share : k * share + requests]
            sq = sq_scr[start : start + requests]
            rows = slice(i * requests, (i + 1) * requests)
            out_ref[k, rows] = jnp.where(mine, own, sq).astype(BF16)


def activate(parts_ref, out_ref, scr):
    copies, double, _ = parts_ref.shape
    requests = double // 2
    share = 9
    total = parts_ref[0].astype(F32)
    for k in range(1, copies):
        total = total + parts_ref[k].astype(F32)
    scr[:double] = total
    scr[double:] = jnp.ones((scr.shape[0] - double, LANES), F32)
    row = iota((requests, LANES), 0)
    squares = jnp.where(
        row < requests - share,
        scr[share : share + requests],
        scr[2 * share : 2 * share + requests],
    )
    scale = lax.rsqrt(squares / D + 1e-06)
    gate_sum = total[:requests] * scale
    up_sum = total[requests:] * scale
    result = jnp.where(row < share, jax.nn.silu(gate_sum) * up_sum, 0.0).astype(BF16)
    for k in range(copies):
        out_ref[k] = result


def project_down(parts_ref, weight_ref, out_ref, scr):
    copies, requests, _ = parts_ref.shape
    share = 9
    for k in range(copies):
        scr[k * share : k * share + requests] = parts_ref[k].astype(F32)
    blocks = weight_ref.shape[1] // LANES
    cols = [scr[c * requests : (c + 1) * requests].astype(BF16) for c in range(blocks)]
    result = dot_nt(jnp.concatenate(cols, axis=1), weight_ref[...])
    for t in range(out_ref.shape[0]):
        out_ref[t] = result


def finish(parts_ref, hidden_ref, out_ref):
    total = hidden_ref[...]
    for t in range(parts_ref.shape[0]):
        total = total + parts_ref[t]
    out_ref[...] = total.astype(BF16)


def run(kernel, outs, scratch, *args, smem=0, limit=16):
    shapes = [jax.ShapeDtypeStruct(shape, dtype) for shape, dtype in outs]
    return pl.pallas_call(
        kernel,
        out_shape=shapes if len(shapes) > 1 else shapes[0],
        in_specs=[SMEM] * smem + [VMEM] * (len(args) - smem),
        out_specs=[VMEM] * len(shapes) if len(shapes) > 1 else VMEM,
        scratch_shapes=[pltpu.VMEM(shape, dtype) for shape, dtype in scratch],
        compiler_params=pltpu.CompilerParams(vmem_limit_bytes=limit * 2**20),
    )(*args)


def exchange(x, axis):
    return lax.all_to_all(x, axis, 0, 0)


def on_device(
    q_nope,
    q_rope,
    w_absorb,
    w_value,
    w_out,
    kv_cache,
    new_latent,
    lengths,
    page_table,
    residual,
    norm_gain,
    w_gate,
    w_up,
    w_down,
):
    requests = q_nope.shape[0]
    heads, nope, latent = w_absorb.shape
    slots, page_len, ctx = kv_cache.shape
    n_kv = lax.axis_size("kv")
    n_tp = lax.axis_size("tp")
    width = residual.shape[1]
    units = w_gate.shape[1]
    scale = 1.0 / math.sqrt(nope + ctx - latent)
    me = lax.axis_index("kv").astype(jnp.int32).reshape(1)

    pages, new = pl.pallas_call(
        functools.partial(attend, scale),
        out_shape=[
            jax.ShapeDtypeStruct((n_kv, slots, LANES), F32),
            jax.ShapeDtypeStruct((requests, LANES), F32),
        ],
        in_specs=[SMEM] + [HBM] * 8,
        out_specs=[VMEM] * 2,
        scratch_shapes=[
            pltpu.SMEM((requests,), jnp.int32),
            pltpu.VMEM(page_table.shape, jnp.int32),
            pltpu.VMEM(q_nope.shape, BF16),
            pltpu.VMEM(q_rope.shape, BF16),
            pltpu.VMEM(w_absorb.shape, BF16),
            pltpu.VMEM((slots, ctx, page_len), BF16),
            pltpu.VMEM(w_value.shape, BF16),
            pltpu.VMEM(new_latent.shape, BF16),
            pltpu.VMEM((latent // LANES + 1, heads * slots, LANES), F32),
            pltpu.VMEM((latent // LANES + 1, heads * slots, LANES), F32),
            pltpu.SemaphoreType.DMA((7,)),
            pltpu.SemaphoreType.DMA((slots,)),
        ],
        compiler_params=pltpu.CompilerParams(vmem_limit_bytes=24 * 2**20),
    )(
        me,
        *(
            pltpu.with_memory_space_constraint(x, pltpu.HBM)
            for x in (
                lengths,
                page_table,
                q_nope,
                q_rope,
                w_absorb,
                jnp.swapaxes(kv_cache, 1, 2),
                w_value,
                new_latent,
            )
        ),
    )
    pages = exchange(pages, "kv").reshape(n_kv * slots, LANES)
    value = run(
        combine, [((n_kv, requests, LANES), BF16)], [], me, page_table, pages, new, smem=1
    )
    value = exchange(value, "kv")
    attention = run(attention_out, [((n_tp, requests, width), F32)], [], value, w_out.T)
    attention = exchange(attention, "tp")
    rows = units // LANES * requests
    sums, hidden = run(
        gate_up,
        [((n_kv, 2 * requests, LANES), BF16), ((requests, width), F32)],
        [((rows + requests, LANES), F32)] * 2 + [((3 * requests, LANES), F32)],
        attention,
        residual,
        norm_gain,
        w_gate,
        w_up,
    )
    sums = exchange(sums, "kv")
    activation = run(
        activate, [((n_kv, requests, LANES), BF16)], [((3 * requests, LANES), F32)], sums
    )
    activation = exchange(activation, "kv")
    down = run(
        project_down,
        [((n_tp, requests, width), F32)],
        [((rows + requests, LANES), F32)],
        activation,
        w_down.T,
    )
    down = exchange(down, "tp")
    return run(finish, [((requests, width), BF16)], [], down, hidden)


def solution(mesh):
    return jax.shard_map(
        on_device,
        mesh=mesh,
        in_specs=(
            P(None, "tp"),
            P(None, "tp"),
            P("tp", None, None),
            P("tp", None, None),
            P("tp", "kv"),
            P("kv", None, None),
            P(),
            P(),
            P(),
            P(None, "kv"),
            P("kv"),
            P("kv", "tp"),
            P("kv", "tp"),
            P("tp", "kv"),
        ),
        out_specs=P(None, "kv"),
        check_vma=False,
    )
```

```python
import functools
import math

import jax
import jax.numpy as jnp
from jax import lax
from jax.experimental import pallas as pl
from jax.experimental.pallas import tpu as pltpu
from jax.sharding import PartitionSpec as P

D = 7168
LOW = -1e30
LANES = 128
SHARE = 9
HALF = LANES // 2
TOTAL = HALF + HALF // 2
THIRD = 8
F32 = jnp.float32
BF16 = jnp.bfloat16
HIGHEST = lax.Precision.HIGHEST
VMEM = pl.BlockSpec(memory_space=pltpu.VMEM)
SMEM = pl.BlockSpec(memory_space=pltpu.SMEM)
HBM = pl.BlockSpec(memory_space=pltpu.HBM)


def dot(a, b, precision=None):
    return jnp.dot(a, b, preferred_element_type=F32, precision=precision)


def dot_nt(a, b):
    return lax.dot_general(a, b, (((1,), (1,)), ((), ())), preferred_element_type=F32)


def dot_tn(a, b):
    return lax.dot_general(a, b, (((0,), (0,)), ((), ())), preferred_element_type=F32)


def iota(shape, dim):
    return lax.broadcasted_iota(jnp.int32, shape, dim)


def swap_halves_if(flag, x):
    return jnp.where(flag == 1, pltpu.roll(x, HALF, 1), x)


def in_thirds(x):
    high = x.astype(BF16).astype(F32)
    middle = (x - high).astype(BF16).astype(F32)
    low = x - high - middle
    place = iota(x.shape, 1) % (HALF // 2) // THIRD
    rest = jnp.where(place == 1, middle, jnp.where(place == 2, low, 0.0))
    return jnp.where(place == 0, high, rest)


def attend(
    scale,
    me_ref,
    lengths_hbm,
    table_hbm,
    q_nope_hbm,
    q_rope_hbm,
    absorb_hbm,
    pages_hbm,
    value_hbm,
    new_hbm,
    out_ref,
    new_out_ref,
    lengths_ref,
    table_ref,
    q_nope_ref,
    q_rope_ref,
    absorb_ref,
    pages_ref,
    value_ref,
    new_ref,
    q_scr,
    acc_scr,
    sems,
):
    heads, nope, latent = absorb_ref.shape
    slots, ctx, page_len = pages_ref.shape
    rope = ctx - latent
    requests = new_ref.shape[0]
    me = me_ref[0]
    lane = iota((slots, LANES), 1)
    blocks = latent // LANES

    def fetch(source, target, sem):
        copy = pltpu.make_async_copy(source, target, sem)
        copy.start()
        return copy

    lengths_in = fetch(lengths_hbm, lengths_ref, sems.at[0])
    table_in = fetch(table_hbm, table_ref, sems.at[1])
    q_nope_in = fetch(q_nope_hbm, q_nope_ref, sems.at[2])
    q_rope_in = fetch(q_rope_hbm, q_rope_ref, sems.at[3])
    new_in = fetch(new_hbm, new_ref, sems.at[4])
    absorb_in = fetch(absorb_hbm, absorb_ref, sems.at[5])
    pages_in = fetch(pages_hbm, pages_ref, sems.at[6])
    value_in = fetch(value_hbm, value_ref, sems.at[7])

    lengths_in.wait()
    table_in.wait()
    table = table_ref[...]
    row = iota(table.shape, 0)
    left = iota(table.shape, 1) * -page_len
    for r in range(requests):
        left = left + jnp.where(row == r, lengths_ref[r], 0)
    left = left.astype(F32)
    owner = jnp.zeros((requests, slots), F32)
    tokens = []
    for s in range(slots):
        match = table == me * slots + s
        column = jnp.max(jnp.where(match, 1.0, 0.0), axis=1, keepdims=True)
        owner = owner + jnp.where(iota(owner.shape, 1) == s, column, 0.0)
        found = jnp.sum(jnp.where(match, left, 0.0), axis=1, keepdims=True)
        tokens.append(jnp.sum(found, axis=0, keepdims=True).astype(jnp.int32))
    owner = owner.astype(BF16)

    q_nope_in.wait()
    q_rope_in.wait()
    picked = dot_tn(owner, q_nope_ref[...]).astype(BF16)
    picked_rope = dot_tn(owner, q_rope_ref[...])
    absorb_in.wait()
    for h in range(heads):
        q_lat = dot(picked[:, h * nope : (h + 1) * nope], absorb_ref[h])
        rows = slice(h * slots, (h + 1) * slots)
        q_lat = q_lat.astype(BF16).astype(F32)
        for c in range(blocks):
            q_scr[c, rows] = q_lat[:, c * LANES : (c + 1) * LANES]
        q_scr[blocks, rows, :rope] = picked_rope[:, h * rope : (h + 1) * rope]
    pages_in.wait()

    new_in.wait()
    head = me // 2
    fresh = new_ref[...]
    q_here = q_nope_ref[:, pl.ds(pl.multiple_of(head * nope, nope), nope)]
    q_lat = dot(q_here, absorb_ref[head]).astype(BF16).astype(F32)
    q_rot = q_rope_ref[:, pl.ds(pl.multiple_of((head // 2) * LANES, LANES), LANES)].astype(F32)
    q_rot = swap_halves_if(head % 2, q_rot)[:, :rope]
    fresh32 = fresh.astype(F32)
    new_score = jnp.sum(q_lat * fresh32[:, :latent], axis=1, keepdims=True)
    new_score = new_score + jnp.sum(q_rot * fresh32[:, latent:], axis=1, keepdims=True)
    new_score = new_score * scale

    all_scores = []
    for s in range(slots):
        every = pl.ds(s, heads, stride=slots)
        q = [q_scr[c, every, :] for c in range(blocks + 1)]
        q = jnp.concatenate(q, axis=1)[:, :ctx].astype(BF16)
        all_scores.append(dot(q, pages_ref[s]))
    stat_lane = iota((heads, LANES), 1)
    all_weights = []
    for s in range(slots):
        live = iota((heads, page_len), 1) < tokens[s]
        scores = jnp.where(live, all_scores[s] * scale, LOW)
        most = jnp.max(scores, axis=1, keepdims=True)
        weights = jnp.where(live, jnp.exp(scores - most), 0.0).astype(BF16)
        total = jnp.sum(weights.astype(F32), axis=1, keepdims=True)
        rows = slice(s * heads, (s + 1) * heads)
        acc_scr[blocks, rows] = jnp.where(stat_lane < TOTAL, most, total)
        all_weights.append(weights)
    for s in range(slots):
        rows = slice(s * heads, (s + 1) * heads)
        acc = dot_nt(all_weights[s], pages_ref[s, :latent, :])
        for c in range(blocks):
            acc_scr[c, rows] = acc[:, c * LANES : (c + 1) * LANES]

    value_in.wait()
    all_valued = []
    for h in range(heads):
        every = pl.ds(h, slots, stride=heads)
        acc = jnp.concatenate([acc_scr[c, every, :] for c in range(blocks)], axis=1)
        high = acc.astype(BF16).astype(F32)
        both = jnp.concatenate([high, acc - high], axis=0).astype(BF16)
        all_valued.append(dot(both, value_ref[h]))
    for h in range(heads):
        valued = all_valued[h][:slots] + all_valued[h][slots:]
        stats = in_thirds(acc_scr[blocks, pl.ds(h, slots, stride=heads), :])
        out_ref[2 * h] = jnp.where(lane < HALF, valued, stats).astype(BF16)
        valued = pltpu.roll(valued, HALF, 1)
        out_ref[2 * h + 1] = jnp.where(lane < HALF, valued, stats).astype(BF16)
    valued = swap_halves_if(me % 2, dot(fresh[:, :latent], value_ref[head]))
    lane = iota(valued.shape, 1)
    stats = jnp.where(lane < TOTAL, new_score, jnp.where(lane == TOTAL, 1.0, 0.0))
    new_out_ref[...] = jnp.where(lane < HALF, valued, stats)


def combine(table_ref, pages_ref, new_ref, out_ref):
    slots = pages_ref.shape[0]
    copies = out_ref.shape[0]
    table = table_ref[...]
    requests = table.shape[0]
    slot = iota((requests, slots), 1)
    owns = slot < 0
    for j in range(table.shape[1]):
        owns = owns | (table[:, j : j + 1] == slot)
    pages = pages_ref[...]
    turned = jnp.transpose(pages.astype(F32))
    most = [turned[HALF + i * THIRD : HALF + i * THIRD + 1, :] for i in range(3)]
    most = jnp.where(owns, most[0] + most[1] + most[2], LOW)
    new = new_ref[...]
    new_score = new[:, HALF : HALF + 1]
    top = jnp.maximum(jnp.max(most, axis=1, keepdims=True), new_score)
    factor = jnp.where(owns, jnp.exp(most - top), 0.0)
    high = factor.astype(BF16)
    low = (factor - high.astype(F32)).astype(BF16)
    sums = dot(high, pages) + dot(low, pages) + jnp.exp(new_score - top) * new
    total = [sums[:, TOTAL + i * THIRD : TOTAL + i * THIRD + 1] for i in range(3)]
    value = sums / (total[0] + total[1] + total[2])
    half = requests // 2
    lane = iota((half, LANES), 1)
    packed = jnp.where(lane < HALF, value[:half], pltpu.roll(value[half:], HALF, 1)).astype(BF16)
    for k in range(copies):
        out_ref[k] = packed


def attention_out(parts_ref, weight_ref, out_ref):
    blocks = []
    for h in range(parts_ref.shape[0] // 2):
        left = parts_ref[2 * h].astype(F32)
        right = parts_ref[2 * h + 1].astype(F32)
        lane = iota(left.shape, 1)
        upper = jnp.where(lane < HALF, left, pltpu.roll(right, HALF, 1))
        lower = jnp.where(lane < HALF, pltpu.roll(left, HALF, 1), right)
        blocks.append(jnp.concatenate([upper, lower], axis=0).astype(BF16))
    result = dot_nt(jnp.concatenate(blocks, axis=1), weight_ref[...]).astype(BF16)
    for t in range(out_ref.shape[0]):
        out_ref[t] = result


def gate_up(
    parts_ref, residual_ref, gain_ref, gate_ref, up_ref, out_ref, hidden_ref, gate_scr, up_scr, out_scr
):
    requests = residual_ref.shape[0]
    copies, height, _ = out_ref.shape
    blocks = gate_ref.shape[1] // LANES
    hidden = residual_ref[...].astype(F32)
    for t in range(parts_ref.shape[0]):
        hidden = hidden + parts_ref[t].astype(F32)
    hidden_ref[...] = hidden
    squares = jnp.sum(hidden * hidden, axis=1, keepdims=True)
    shape = (requests, LANES)
    diagonal = iota(shape, 0) == iota(shape, 1) % requests
    squares = jnp.sum(jnp.where(diagonal, squares, 0.0), axis=0, keepdims=True)
    high = squares.astype(BF16).astype(F32)
    row = iota((8, LANES), 0)
    squares = jnp.where(row == 0, high, jnp.where(row == 1, squares - high, 0.0))
    gained = (hidden * gain_ref[...].astype(F32)[None, :]).astype(BF16)
    for weight_ref, scr in ((gate_ref, gate_scr), (up_ref, up_scr)):
        part = dot(gained, weight_ref[...])
        for c in range(blocks):
            scr[c * requests : (c + 1) * requests] = part[:, c * LANES : (c + 1) * LANES]
    for k in range(copies):
        start = k * height
        own = slice(k * SHARE, k * SHARE + requests)
        out_scr[start : start + requests] = gate_scr[own]
        out_scr[start + SHARE : start + SHARE + requests] = up_scr[own]
        out_scr[start + 2 * SHARE : start + 2 * SHARE + 8] = squares
    for k in range(copies):
        out_ref[k] = out_scr[k * height : (k + 1) * height].astype(BF16)


def activate(me_ref, parts_ref, out_ref, scr):
    copies, requests, _ = out_ref.shape
    height = parts_ref.shape[1]
    total = parts_ref[0].astype(F32)
    for k in range(1, copies):
        total = total + parts_ref[k].astype(F32)
    scr[:height] = total
    row = iota((requests, LANES), 0)
    mine = iota(row.shape, 1) == (me_ref[0] * SHARE + row) % requests
    squares = scr[2 * SHARE : 2 * SHARE + 1] + scr[2 * SHARE + 1 : 2 * SHARE + 2]
    squares = jnp.sum(jnp.where(mine, squares, 0.0), axis=1, keepdims=True)
    scale = lax.rsqrt(squares / D + 1e-06)
    gate_sum = total[:requests] * scale
    up_sum = scr[SHARE : SHARE + requests] * scale
    result = jnp.where(row < SHARE, jax.nn.silu(gate_sum) * up_sum, 0.0).astype(BF16)
    for k in range(copies):
        out_ref[k] = result


def project_down(parts_ref, weight_ref, out_ref, scr):
    copies, requests, _ = parts_ref.shape
    for k in range(copies):
        scr[k * SHARE : k * SHARE + requests] = parts_ref[k].astype(F32)
    blocks = weight_ref.shape[1] // LANES
    cols = [scr[c * requests : (c + 1) * requests].astype(BF16) for c in range(blocks)]
    result = dot_nt(jnp.concatenate(cols, axis=1), weight_ref[...]).astype(BF16)
    for t in range(out_ref.shape[0]):
        out_ref[t] = result


def finish(parts_ref, hidden_ref, out_ref):
    total = hidden_ref[...]
    for t in range(parts_ref.shape[0]):
        total = total + parts_ref[t].astype(F32)
    out_ref[...] = total.astype(BF16)


def run(kernel, outs, scratch, *args, smem=0, limit=16):
    shapes = [jax.ShapeDtypeStruct(shape, dtype) for shape, dtype in outs]
    return pl.pallas_call(
        kernel,
        out_shape=shapes if len(shapes) > 1 else shapes[0],
        in_specs=[SMEM] * smem + [VMEM] * (len(args) - smem),
        out_specs=[VMEM] * len(shapes) if len(shapes) > 1 else VMEM,
        scratch_shapes=[pltpu.VMEM(shape, dtype) for shape, dtype in scratch],
        compiler_params=pltpu.CompilerParams(vmem_limit_bytes=limit * 2**20),
    )(*args)


def exchange(x, axis):
    return lax.all_to_all(x, axis, 0, 0)


def on_device(
    q_nope,
    q_rope,
    w_absorb,
    w_value,
    w_out,
    kv_cache,
    new_latent,
    lengths,
    page_table,
    residual,
    norm_gain,
    w_gate,
    w_up,
    w_down,
):
    requests = q_nope.shape[0]
    heads, nope, latent = w_absorb.shape
    slots, page_len, ctx = kv_cache.shape
    n_kv = lax.axis_size("kv")
    n_tp = lax.axis_size("tp")
    width = residual.shape[1]
    units = w_gate.shape[1]
    scale = 1.0 / math.sqrt(nope + ctx - latent)
    me = lax.axis_index("kv").astype(jnp.int32).reshape(1)

    pages, new = pl.pallas_call(
        functools.partial(attend, scale),
        out_shape=[
            jax.ShapeDtypeStruct((n_kv, slots, LANES), BF16),
            jax.ShapeDtypeStruct((requests, LANES), F32),
        ],
        in_specs=[SMEM] + [HBM] * 8,
        out_specs=[VMEM] * 2,
        scratch_shapes=[
            pltpu.SMEM((requests,), jnp.int32),
            pltpu.VMEM(page_table.shape, jnp.int32),
            pltpu.VMEM(q_nope.shape, BF16),
            pltpu.VMEM(q_rope.shape, BF16),
            pltpu.VMEM(w_absorb.shape, BF16),
            pltpu.VMEM((slots, ctx, page_len), BF16),
            pltpu.VMEM(w_value.shape, BF16),
            pltpu.VMEM(new_latent.shape, BF16),
            pltpu.VMEM((latent // LANES + 1, heads * slots, LANES), F32),
            pltpu.VMEM((latent // LANES + 1, heads * slots, LANES), F32),
            pltpu.SemaphoreType.DMA((8,)),
        ],
        compiler_params=pltpu.CompilerParams(vmem_limit_bytes=24 * 2**20),
    )(
        me,
        *(
            pltpu.with_memory_space_constraint(x, pltpu.HBM)
            for x in (
                lengths,
                page_table,
                q_nope,
                q_rope,
                w_absorb,
                jnp.swapaxes(kv_cache, 1, 2),
                w_value,
                new_latent,
            )
        ),
    )
    pages = exchange(pages, "kv").reshape(n_kv * slots, LANES)
    value = run(
        combine, [((n_kv, requests // 2, LANES), BF16)], [], page_table, pages, new
    )
    value = exchange(value, "kv")
    attention = run(attention_out, [((n_tp, requests, width), BF16)], [], value, w_out.T)
    attention = exchange(attention, "tp")
    rows = units // LANES * requests
    height = 24
    sums, hidden = run(
        gate_up,
        [((n_kv, height, LANES), BF16), ((requests, width), F32)],
        [((rows + requests, LANES), F32)] * 2 + [((n_kv * height + 8, LANES), F32)],
        attention,
        residual,
        norm_gain,
        w_gate,
        w_up,
    )
    sums = exchange(sums, "kv")
    activation = run(
        activate, [((n_kv, requests, LANES), BF16)], [((height + 8, LANES), F32)], me, sums, smem=1
    )
    activation = exchange(activation, "kv")
    down = run(
        project_down,
        [((n_tp, requests, width), BF16)],
        [((rows + requests, LANES), F32)],
        activation,
        w_down.T,
    )
    down = exchange(down, "tp")
    return run(finish, [((requests, width), BF16)], [], down, hidden)


def solution(mesh):
    return jax.shard_map(
        on_device,
        mesh=mesh,
        in_specs=(
            P(None, "tp"),
            P(None, "tp"),
            P("tp", None, None),
            P("tp", None, None),
            P("tp", "kv"),
            P("kv", None, None),
            P(),
            P(),
            P(),
            P(None, "kv"),
            P("kv"),
            P("kv", "tp"),
            P("kv", "tp"),
            P("tp", "kv"),
        ),
        out_specs=P(None, "kv"),
        check_vma=False,
    )
```

```python
import functools
import math

import jax
import jax.numpy as jnp
from jax import lax
from jax.experimental import pallas as pl
from jax.experimental.pallas import tpu as pltpu
from jax.sharding import PartitionSpec as P

D = 7168
LOW = -1e30
LANES = 128
CLASSES = 8
SHARE = 9
STATS = 6
F32 = jnp.float32
BF16 = jnp.bfloat16
HIGHEST = lax.Precision.HIGHEST
VMEM = pl.BlockSpec(memory_space=pltpu.VMEM)
SMEM = pl.BlockSpec(memory_space=pltpu.SMEM)
HBM = pl.BlockSpec(memory_space=pltpu.HBM)


def dot(a, b, precision=None):
    return jnp.dot(a, b, preferred_element_type=F32, precision=precision)


def dot_nt(a, b):
    return lax.dot_general(a, b, (((1,), (1,)), ((), ())), preferred_element_type=F32)


def dot_tn(a, b):
    return lax.dot_general(a, b, (((0,), (0,)), ((), ())), preferred_element_type=F32)


def iota(shape, dim):
    return lax.broadcasted_iota(jnp.int32, shape, dim)


def in_thirds(x):
    high = x.astype(BF16).astype(F32)
    middle = (x - high).astype(BF16).astype(F32)
    low = x - high - middle
    place = iota(x.shape, 1) % 3
    return jnp.where(place == 0, high, jnp.where(place == 1, middle, low))


def attend(
    scale,
    me_ref,
    lengths_hbm,
    table_hbm,
    q_nope_hbm,
    q_rope_hbm,
    absorb_hbm,
    pages_hbm,
    value_hbm,
    new_hbm,
    out_ref,
    new_out_ref,
    lengths_ref,
    table_ref,
    q_nope_ref,
    q_rope_ref,
    absorb_ref,
    pages_ref,
    value_ref,
    new_ref,
    q_scr,
    acc_scr,
    sems,
):
    heads, nope, latent = absorb_ref.shape
    slots, ctx, page_len = pages_ref.shape
    rope = ctx - latent
    requests = new_ref.shape[0]
    me = me_ref[0]
    blocks = latent // LANES

    def fetch(source, target, sem):
        copy = pltpu.make_async_copy(source, target, sem)
        copy.start()
        return copy

    lengths_in = fetch(lengths_hbm, lengths_ref, sems.at[0])
    table_in = fetch(table_hbm, table_ref, sems.at[1])
    q_nope_in = fetch(q_nope_hbm, q_nope_ref, sems.at[2])
    q_rope_in = fetch(q_rope_hbm, q_rope_ref, sems.at[3])
    new_in = fetch(new_hbm, new_ref, sems.at[4])
    absorb_in = fetch(absorb_hbm, absorb_ref, sems.at[5])
    pages_in = fetch(pages_hbm, pages_ref, sems.at[6])
    value_in = fetch(value_hbm, value_ref, sems.at[7])

    lengths_in.wait()
    table_in.wait()
    table = table_ref[...]
    row = iota(table.shape, 0)
    left = iota(table.shape, 1) * -page_len
    for r in range(requests):
        left = left + jnp.where(row == r, lengths_ref[r], 0)
    left = left.astype(F32)
    owner = jnp.zeros((requests, slots), F32)
    tokens = []
    for s in range(slots):
        match = table == me * slots + s
        column = jnp.max(jnp.where(match, 1.0, 0.0), axis=1, keepdims=True)
        owner = owner + jnp.where(iota(owner.shape, 1) == s, column, 0.0)
        found = jnp.sum(jnp.where(match, left, 0.0), axis=1, keepdims=True)
        tokens.append(jnp.sum(found, axis=0, keepdims=True).astype(jnp.int32))
    owner = owner.astype(BF16)

    q_nope_in.wait()
    q_rope_in.wait()
    new_in.wait()
    fresh = new_ref[...].astype(F32)
    fresh_rope = jnp.concatenate([fresh[:, latent:]] * 2, axis=1)
    q_nope = jnp.concatenate(
        [dot_tn(owner, q_nope_ref[...]), q_nope_ref[...].astype(F32)], axis=0
    ).astype(BF16)
    picked_rope = dot_tn(owner, q_rope_ref[...])
    first_half = iota((requests, LANES), 1) < rope
    absorb_in.wait()
    for h in range(heads):
        q_lat = dot(q_nope[:, h * nope : (h + 1) * nope], absorb_ref[h])
        q_lat = q_lat.astype(BF16).astype(F32)
        rows = slice(h * slots, (h + 1) * slots)
        pair = slice(h // 2 * LANES, (h // 2 + 1) * LANES)
        products = q_rope_ref[:, pair].astype(F32) * fresh_rope
        products = jnp.where(first_half == (h % 2 == 0), products, 0.0)
        for c in range(blocks):
            lanes = slice(c * LANES, (c + 1) * LANES)
            q_scr[c, rows] = q_lat[:slots, lanes]
            products = products + q_lat[slots:, lanes] * fresh[:, lanes]
        q_scr[blocks, rows, :rope] = picked_rope[:, h * rope : (h + 1) * rope]
        new_score = jnp.sum(products, axis=1, keepdims=True) * scale
        new_out_ref[h, :, LANES:] = jnp.broadcast_to(new_score, (requests, LANES))
    pages_in.wait()

    all_scores = []
    for s in range(slots):
        every = pl.ds(s, heads, stride=slots)
        q = [q_scr[c, every, :] for c in range(blocks + 1)]
        q = jnp.concatenate(q, axis=1)[:, :ctx].astype(BF16)
        all_scores.append(dot(q, pages_ref[s]))
    all_weights = []
    for s in range(slots):
        live = iota((heads, page_len), 1) < tokens[s]
        scores = jnp.where(live, all_scores[s] * scale, LOW)
        most = jnp.max(scores, axis=1, keepdims=True)
        weights = jnp.where(live, jnp.exp(scores - most), 0.0).astype(BF16)
        total = jnp.sum(weights.astype(F32), axis=1, keepdims=True)
        rows = slice(s * heads, (s + 1) * heads)
        acc_scr[blocks, rows] = jnp.broadcast_to(most, (heads, LANES))
        acc_scr[blocks + 1, rows] = jnp.broadcast_to(total, (heads, LANES))
        all_weights.append(weights)
    for s in range(slots):
        rows = slice(s * heads, (s + 1) * heads)
        acc = dot_nt(all_weights[s], pages_ref[s, :latent, :])
        for c in range(blocks):
            acc_scr[c, rows] = acc[:, c * LANES : (c + 1) * LANES]

    value_in.wait()
    all_valued = []
    for h in range(heads):
        every = pl.ds(h, slots, stride=heads)
        acc = jnp.concatenate([acc_scr[c, every, :] for c in range(blocks)], axis=1)
        high = acc.astype(BF16).astype(F32)
        rows = jnp.concatenate([high, acc - high, fresh[:, :latent]], axis=0).astype(BF16)
        all_valued.append(dot(rows, value_ref[h]))
    copies = out_ref.shape[0]
    share = heads // CLASSES
    lane = iota((slots, LANES), 1)
    for part in range(CLASSES):
        stats = jnp.zeros((slots, LANES), F32)
        rows = []
        for i in range(share):
            h = part * share + i
            every = pl.ds(h, slots, stride=heads)
            stat = jnp.where(
                lane % STATS < 3, acc_scr[blocks, every, :], acc_scr[blocks + 1, every, :]
            )
            stats = jnp.where(lane // STATS == i, stat, stats)
            rows.append(all_valued[h][:slots] + all_valued[h][slots : 2 * slots])
            new_out_ref[h, :, :LANES] = all_valued[h][2 * slots :]
        rows = jnp.concatenate(rows + [in_thirds(stats)], axis=0).astype(BF16)
        for k in range(part, copies, CLASSES):
            out_ref[k] = rows


def combine(me_ref, table_ref, parts_ref, new_ref, out_ref):
    sources, height, _ = parts_ref.shape
    heads, requests, _ = new_ref.shape
    share = heads // CLASSES
    slots_each = height // (share + 1)
    slots = sources * slots_each
    first = me_ref[0] % CLASSES * share
    table = table_ref[...]
    slot = iota((requests, slots), 1)
    owns = slot < 0
    for j in range(table.shape[1]):
        owns = owns | (table[:, j : j + 1] == slot)

    def rows_of(i):
        rows = parts_ref[:, i * slots_each : (i + 1) * slots_each, :]
        return rows.astype(F32).reshape(slots, LANES).astype(BF16)

    stats = rows_of(share)
    row = iota((share * requests, LANES), 0) // requests
    lane = iota((share * requests, LANES), 1)
    thirds = (lane // STATS == row) & (lane % STATS < 3)
    most = dot_nt(jnp.where(thirds, 1.0, 0.0).astype(BF16), stats)
    factors, keeps = [], []
    for i in range(share):
        page_max = jnp.where(owns, most[i * requests : (i + 1) * requests], LOW)
        new_score = new_ref[first + i, :, LANES:]
        top = jnp.maximum(jnp.max(page_max, axis=1, keepdims=True), new_score)
        factor = jnp.where(owns, jnp.exp(page_max - top[:, :1]), 0.0)
        high = factor.astype(BF16).astype(F32)
        factors.append(jnp.concatenate([high, factor - high], axis=0).astype(BF16))
        keeps.append(jnp.exp(new_score - top))
    sums = [
        dot(factors[i], jnp.concatenate([rows_of(i), stats], axis=1)) for i in range(share)
    ]
    lane = iota((requests, LANES), 1)
    values = []
    for i in range(share):
        both = sums[i][:requests] + sums[i][requests:]
        mine = (lane // STATS == i) & (lane % STATS >= 3)
        total = jnp.sum(jnp.where(mine, both[:, LANES:], 0.0), axis=1, keepdims=True)
        value = both[:, :LANES] + keeps[i] * new_ref[first + i, :, :LANES]
        values.append((value / (total + keeps[i])).astype(BF16))
    values = jnp.concatenate(values, axis=1)
    for k in range(CLASSES):
        out_ref[k] = values


def attention_out(parts_ref, weight_ref, out_ref):
    value = jnp.concatenate([parts_ref[k] for k in range(parts_ref.shape[0])], axis=1)
    result = dot_nt(value, weight_ref[...]).astype(BF16)
    for t in range(out_ref.shape[0]):
        out_ref[t] = result


def gate_up(
    parts_ref, residual_ref, gain_ref, gate_ref, up_ref, out_ref, hidden_ref, gate_scr, up_scr, out_scr
):
    requests = residual_ref.shape[0]
    copies, height, _ = out_ref.shape
    blocks = gate_ref.shape[1] // LANES
    hidden = residual_ref[...].astype(F32)
    for t in range(parts_ref.shape[0]):
        hidden = hidden + parts_ref[t].astype(F32)
    hidden_ref[...] = hidden
    squares = jnp.sum(hidden * hidden, axis=1, keepdims=True)
    shape = (requests, LANES)
    diagonal = iota(shape, 0) == iota(shape, 1) % requests
    squares = jnp.sum(jnp.where(diagonal, squares, 0.0), axis=0, keepdims=True)
    high = squares.astype(BF16).astype(F32)
    row = iota((8, LANES), 0)
    squares = jnp.where(row == 0, high, jnp.where(row == 1, squares - high, 0.0))
    gained = (hidden * gain_ref[...].astype(F32)[None, :]).astype(BF16)
    for weight_ref, scr in ((gate_ref, gate_scr), (up_ref, up_scr)):
        part = dot(gained, weight_ref[...])
        for c in range(blocks):
            scr[c * requests : (c + 1) * requests] = part[:, c * LANES : (c + 1) * LANES]
    for k in range(copies):
        start = k * height
        own = slice(k * SHARE, k * SHARE + requests)
        out_scr[start : start + requests] = gate_scr[own]
        out_scr[start + SHARE : start + SHARE + requests] = up_scr[own]
        out_scr[start + 2 * SHARE : start + 2 * SHARE + 8] = squares
    for k in range(copies):
        out_ref[k] = out_scr[k * height : (k + 1) * height].astype(BF16)


def activate(me_ref, parts_ref, out_ref, scr):
    copies, requests, _ = out_ref.shape
    height = parts_ref.shape[1]
    total = parts_ref[0].astype(F32)
    for k in range(1, copies):
        total = total + parts_ref[k].astype(F32)
    scr[:height] = total
    row = iota((requests, LANES), 0)
    mine = iota(row.shape, 1) == (me_ref[0] * SHARE + row) % requests
    squares = scr[2 * SHARE : 2 * SHARE + 1] + scr[2 * SHARE + 1 : 2 * SHARE + 2]
    squares = jnp.sum(jnp.where(mine, squares, 0.0), axis=1, keepdims=True)
    scale = lax.rsqrt(squares / D + 1e-06)
    gate_sum = total[:requests] * scale
    up_sum = scr[SHARE : SHARE + requests] * scale
    result = jnp.where(row < SHARE, jax.nn.silu(gate_sum) * up_sum, 0.0).astype(BF16)
    for k in range(copies):
        out_ref[k] = result


def project_down(parts_ref, weight_ref, out_ref, scr):
    copies, requests, _ = parts_ref.shape
    for k in range(copies):
        scr[k * SHARE : k * SHARE + requests] = parts_ref[k].astype(F32)
    blocks = weight_ref.shape[1] // LANES
    cols = [scr[c * requests : (c + 1) * requests].astype(BF16) for c in range(blocks)]
    result = dot_nt(jnp.concatenate(cols, axis=1), weight_ref[...]).astype(BF16)
    for t in range(out_ref.shape[0]):
        out_ref[t] = result


def finish(parts_ref, hidden_ref, out_ref):
    total = hidden_ref[...]
    for t in range(parts_ref.shape[0]):
        total = total + parts_ref[t].astype(F32)
    out_ref[...] = total.astype(BF16)


def run(kernel, outs, scratch, *args, smem=0, limit=16):
    shapes = [jax.ShapeDtypeStruct(shape, dtype) for shape, dtype in outs]
    return pl.pallas_call(
        kernel,
        out_shape=shapes if len(shapes) > 1 else shapes[0],
        in_specs=[SMEM] * smem + [VMEM] * (len(args) - smem),
        out_specs=[VMEM] * len(shapes) if len(shapes) > 1 else VMEM,
        scratch_shapes=[pltpu.VMEM(shape, dtype) for shape, dtype in scratch],
        compiler_params=pltpu.CompilerParams(vmem_limit_bytes=limit * 2**20),
    )(*args)


def exchange(x, axis, groups=None):
    return lax.all_to_all(x, axis, 0, 0, axis_index_groups=groups)


def on_device(
    q_nope,
    q_rope,
    w_absorb,
    w_value,
    w_out,
    kv_cache,
    new_latent,
    lengths,
    page_table,
    residual,
    norm_gain,
    w_gate,
    w_up,
    w_down,
):
    requests = q_nope.shape[0]
    heads, nope, latent = w_absorb.shape
    slots, page_len, ctx = kv_cache.shape
    n_kv = lax.axis_size("kv")
    n_tp = lax.axis_size("tp")
    width = residual.shape[1]
    units = w_gate.shape[1]
    scale = 1.0 / math.sqrt(nope + ctx - latent)
    me = lax.axis_index("kv").astype(jnp.int32).reshape(1)

    pages, new = pl.pallas_call(
        functools.partial(attend, scale),
        out_shape=[
            jax.ShapeDtypeStruct((n_kv, slots * (heads // CLASSES + 1), LANES), BF16),
            jax.ShapeDtypeStruct((heads, requests, 2 * LANES), F32),
        ],
        in_specs=[SMEM] + [HBM] * 8,
        out_specs=[VMEM] * 2,
        scratch_shapes=[
            pltpu.SMEM((requests,), jnp.int32),
            pltpu.VMEM(page_table.shape, jnp.int32),
            pltpu.VMEM(q_nope.shape, BF16),
            pltpu.VMEM(q_rope.shape, BF16),
            pltpu.VMEM(w_absorb.shape, BF16),
            pltpu.VMEM((slots, ctx, page_len), BF16),
            pltpu.VMEM(w_value.shape, BF16),
            pltpu.VMEM(new_latent.shape, BF16),
            pltpu.VMEM((latent // LANES + 1, heads * slots, LANES), F32),
            pltpu.VMEM((latent // LANES + 2, heads * slots, LANES), F32),
            pltpu.SemaphoreType.DMA((8,)),
        ],
        compiler_params=pltpu.CompilerParams(vmem_limit_bytes=24 * 2**20),
    )(
        me,
        *(
            pltpu.with_memory_space_constraint(x, pltpu.HBM)
            for x in (
                lengths,
                page_table,
                q_nope,
                q_rope,
                w_absorb,
                jnp.swapaxes(kv_cache, 1, 2),
                w_value,
                new_latent,
            )
        ),
    )
    pages = exchange(pages, "kv")
    value = run(
        combine,
        [((CLASSES, requests, heads // CLASSES * LANES), BF16)],
        [],
        me,
        page_table,
        pages,
        new,
        smem=1,
    )
    groups = [list(range(k, k + CLASSES)) for k in range(0, n_kv, CLASSES)]
    value = exchange(value, "kv", groups)
    attention = run(attention_out, [((n_tp, requests, width), BF16)], [], value, w_out.T)
    attention = exchange(attention, "tp")
    rows = units // LANES * requests
    height = 24
    sums, hidden = run(
        gate_up,
        [((n_kv, height, LANES), BF16), ((requests, width), F32)],
        [((rows + requests, LANES), F32)] * 2 + [((n_kv * height + 8, LANES), F32)],
        attention,
        residual,
        norm_gain,
        w_gate,
        w_up,
    )
    sums = exchange(sums, "kv")
    activation = run(
        activate, [((n_kv, requests, LANES), BF16)], [((height + 8, LANES), F32)], me, sums, smem=1
    )
    activation = exchange(activation, "kv")
    down = run(
        project_down,
        [((n_tp, requests, width), BF16)],
        [((rows + requests, LANES), F32)],
        activation,
        w_down.T,
    )
    down = exchange(down, "tp")
    return run(finish, [((requests, width), BF16)], [], down, hidden)


def solution(mesh):
    return jax.shard_map(
        on_device,
        mesh=mesh,
        in_specs=(
            P(None, "tp"),
            P(None, "tp"),
            P("tp", None, None),
            P("tp", None, None),
            P("tp", "kv"),
            P("kv", None, None),
            P(),
            P(),
            P(),
            P(None, "kv"),
            P("kv"),
            P("kv", "tp"),
            P("kv", "tp"),
            P("tp", "kv"),
        ),
        out_specs=P(None, "kv"),
        check_vma=False,
    )
```

```python
import functools
import math

import jax
import jax.numpy as jnp
from jax import lax
from jax.experimental import pallas as pl
from jax.experimental.pallas import tpu as pltpu
from jax.sharding import PartitionSpec as P

D = 7168
LOW = -1e30
LANES = 128
CLASSES = 8
REQUESTS = 16
SHARE = 9
STATS = 6
F32 = jnp.float32
BF16 = jnp.bfloat16
HIGHEST = lax.Precision.HIGHEST
VMEM = pl.BlockSpec(memory_space=pltpu.VMEM)
SMEM = pl.BlockSpec(memory_space=pltpu.SMEM)
HBM = pl.BlockSpec(memory_space=pltpu.HBM)


def dot(a, b, precision=None):
    return jnp.dot(a, b, preferred_element_type=F32, precision=precision)


def dot_nt(a, b):
    return lax.dot_general(a, b, (((1,), (1,)), ((), ())), preferred_element_type=F32)


def dot_tn(a, b):
    return lax.dot_general(a, b, (((0,), (0,)), ((), ())), preferred_element_type=F32)


def iota(shape, dim):
    return lax.broadcasted_iota(jnp.int32, shape, dim)


def in_thirds(x):
    high = x.astype(BF16).astype(F32)
    middle = (x - high).astype(BF16).astype(F32)
    low = x - high - middle
    place = iota(x.shape, 1) % 3
    return jnp.where(place == 0, high, jnp.where(place == 1, middle, low))


def attend(
    scale,
    me_ref,
    lengths_hbm,
    table_hbm,
    q_nope_hbm,
    q_rope_hbm,
    absorb_hbm,
    pages_hbm,
    value_hbm,
    new_hbm,
    out_ref,
    new_out_ref,
    lengths_ref,
    table_ref,
    q_nope_ref,
    q_rope_ref,
    absorb_ref,
    pages_ref,
    value_ref,
    new_ref,
    q_scr,
    acc_scr,
    sems,
):
    heads, nope, latent = absorb_ref.shape
    slots, ctx, page_len = pages_ref.shape
    rope = ctx - latent
    requests = new_ref.shape[0]
    me = me_ref[0]
    blocks = latent // LANES

    def fetch(source, target, sem):
        copy = pltpu.make_async_copy(source, target, sem)
        copy.start()
        return copy

    lengths_in = fetch(lengths_hbm, lengths_ref, sems.at[0])
    table_in = fetch(table_hbm, table_ref, sems.at[1])
    q_nope_in = fetch(q_nope_hbm, q_nope_ref, sems.at[2])
    q_rope_in = fetch(q_rope_hbm, q_rope_ref, sems.at[3])
    new_in = fetch(new_hbm, new_ref, sems.at[4])
    absorb_in = fetch(absorb_hbm, absorb_ref, sems.at[5])
    pages_in = fetch(pages_hbm, pages_ref, sems.at[6])
    value_in = fetch(value_hbm, value_ref, sems.at[7])

    lengths_in.wait()
    table_in.wait()
    table = table_ref[...]
    row = iota(table.shape, 0)
    left = iota(table.shape, 1) * -page_len
    for r in range(requests):
        left = left + jnp.where(row == r, lengths_ref[r], 0)
    left = left.astype(F32)
    owner = jnp.zeros((requests, slots), F32)
    tokens = []
    for s in range(slots):
        match = table == me * slots + s
        column = jnp.max(jnp.where(match, 1.0, 0.0), axis=1, keepdims=True)
        owner = owner + jnp.where(iota(owner.shape, 1) == s, column, 0.0)
        found = jnp.sum(jnp.where(match, left, 0.0), axis=1, keepdims=True)
        tokens.append(jnp.sum(found, axis=0, keepdims=True).astype(jnp.int32))
    owner = owner.astype(BF16)

    q_nope_in.wait()
    q_rope_in.wait()
    new_in.wait()
    fresh = new_ref[...].astype(F32)
    fresh_rope = jnp.concatenate([fresh[:, latent:]] * 2, axis=1)
    q_nope = jnp.concatenate(
        [dot_tn(owner, q_nope_ref[...]), q_nope_ref[...].astype(F32)], axis=0
    ).astype(BF16)
    picked_rope = dot_tn(owner, q_rope_ref[...])
    first_half = iota((requests, LANES), 1) < rope
    absorb_in.wait()
    for h in range(heads):
        q_lat = dot(q_nope[:, h * nope : (h + 1) * nope], absorb_ref[h])
        q_lat = q_lat.astype(BF16).astype(F32)
        rows = slice(h * slots, (h + 1) * slots)
        pair = slice(h // 2 * LANES, (h // 2 + 1) * LANES)
        products = q_rope_ref[:, pair].astype(F32) * fresh_rope
        products = jnp.where(first_half == (h % 2 == 0), products, 0.0)
        for c in range(blocks):
            lanes = slice(c * LANES, (c + 1) * LANES)
            q_scr[c, rows] = q_lat[:slots, lanes]
            products = products + q_lat[slots:, lanes] * fresh[:, lanes]
        q_scr[blocks, rows, :rope] = picked_rope[:, h * rope : (h + 1) * rope]
        new_score = jnp.sum(products, axis=1, keepdims=True) * scale
        new_out_ref[h, :, LANES:] = jnp.broadcast_to(new_score, (requests, LANES))
    pages_in.wait()

    all_scores = []
    for s in range(slots):
        every = pl.ds(s, heads, stride=slots)
        q = [q_scr[c, every, :] for c in range(blocks + 1)]
        q = jnp.concatenate(q, axis=1)[:, :ctx].astype(BF16)
        all_scores.append(dot(q, pages_ref[s]))
    all_weights = []
    for s in range(slots):
        live = iota((heads, page_len), 1) < tokens[s]
        scores = jnp.where(live, all_scores[s] * scale, LOW)
        most = jnp.max(scores, axis=1, keepdims=True)
        weights = jnp.where(live, jnp.exp(scores - most), 0.0).astype(BF16)
        total = jnp.sum(weights.astype(F32), axis=1, keepdims=True)
        rows = slice(s * heads, (s + 1) * heads)
        acc_scr[blocks, rows] = jnp.broadcast_to(most, (heads, LANES))
        acc_scr[blocks + 1, rows] = jnp.broadcast_to(total, (heads, LANES))
        all_weights.append(weights)
    for s in range(slots):
        rows = slice(s * heads, (s + 1) * heads)
        acc = dot_nt(all_weights[s], pages_ref[s, :latent, :])
        for c in range(blocks):
            acc_scr[c, rows] = acc[:, c * LANES : (c + 1) * LANES]

    value_in.wait()
    all_valued = []
    for h in range(heads):
        every = pl.ds(h, slots, stride=heads)
        acc = jnp.concatenate([acc_scr[c, every, :] for c in range(blocks)], axis=1)
        high = acc.astype(BF16).astype(F32)
        rows = jnp.concatenate([high, acc - high, fresh[:, :latent]], axis=0).astype(BF16)
        all_valued.append(dot(rows, value_ref[h]))
    for h in range(heads):
        new_out_ref[h, :, :LANES] = all_valued[h][2 * slots :]
    copies, pairs = out_ref.shape[:2]
    share = heads // CLASSES
    row = iota((slots, LANES), 0)
    lane = iota((slots, LANES), 1)
    for part in range(CLASSES):
        stats = jnp.zeros((slots, LANES), F32)
        rows = []
        for i in range(share):
            h = part * share + i
            every = pl.ds(h, slots, stride=heads)
            stat = jnp.where(
                lane % STATS < 3, acc_scr[blocks, every, :], acc_scr[blocks + 1, every, :]
            )
            stat = jnp.where(lane // STATS == row, stat, 0.0)
            stats = jnp.where(row == i, jnp.sum(stat, axis=0, keepdims=True), stats)
            rows.append(all_valued[h][:slots] + all_valued[h][slots : 2 * slots])
        rows = jnp.concatenate(rows + [in_thirds(stats)], axis=0)
        for i in range(pairs):
            pair = rows[2 * i : 2 * i + 2].astype(BF16)
            for k in range(part, copies, CLASSES):
                out_ref[k, i] = pair


def combine(me_ref, table_ref, parts_ref, new_ref, out_ref, acc_scr, stat_scr):
    sources, pairs = parts_ref.shape[:2]
    heads, requests, _ = new_ref.shape
    share = heads // CLASSES
    slots = acc_scr.shape[1]
    slots_each = slots // sources
    first = me_ref[0] % CLASSES * share
    for k in range(sources):
        for i in range(pairs - 1):
            start = k * slots_each + 2 * i % slots_each
            acc_scr[2 * i // slots_each, start : start + 2] = parts_ref[k, i].astype(F32)
        stat_scr[2 * k : 2 * k + 2] = parts_ref[k, pairs - 1].astype(F32)

    stats = stat_scr[...].astype(BF16)
    place = iota((LANES, slots), 0)
    here = place // STATS == iota((LANES, slots), 1) % slots_each
    top_lanes = jnp.where(here & (place % STATS < 3), 1.0, 0.0).astype(BF16)
    sum_lanes = jnp.where(here & (place % STATS >= 3), 1.0, 0.0).astype(BF16)
    top_rows = dot(stats, top_lanes)
    sum_rows = dot(stats, sum_lanes)
    row = iota(top_rows.shape, 0)
    source = iota(top_rows.shape, 1) // slots_each

    table = table_ref[...]
    slot = iota((requests, slots), 1)
    owns = slot < 0
    for j in range(table.shape[1]):
        owns = owns | (table[:, j : j + 1] == slot)

    factors, keeps, totals = [], [], []
    for i in range(share):
        mine = row == 2 * source + i
        page_max = jnp.sum(jnp.where(mine, top_rows, 0.0), axis=0, keepdims=True)
        page_sum = jnp.sum(jnp.where(mine, sum_rows, 0.0), axis=0, keepdims=True)
        page_max = jnp.where(owns, page_max, LOW)
        new_score = new_ref[first + i, :, LANES:]
        top = jnp.maximum(jnp.max(page_max, axis=1, keepdims=True), new_score)
        factor = jnp.where(owns, jnp.exp(page_max - top[:, :1]), 0.0)
        totals.append(jnp.sum(factor * page_sum, axis=1, keepdims=True))
        high = factor.astype(BF16).astype(F32)
        factors.append(jnp.concatenate([high, factor - high], axis=0).astype(BF16))
        keeps.append(jnp.exp(new_score - top))
    sums = [dot(factors[i], acc_scr[i].astype(BF16)) for i in range(share)]
    values = []
    for i in range(share):
        both = sums[i][:requests] + sums[i][requests:]
        value = both + keeps[i] * new_ref[first + i, :, :LANES]
        values.append((value / (totals[i] + keeps[i])).astype(BF16))
    values = jnp.concatenate(values, axis=1)
    for k in range(CLASSES):
        out_ref[k] = values


def attention_out(parts_ref, weight_ref, out_ref):
    value = jnp.concatenate([parts_ref[k] for k in range(parts_ref.shape[0])], axis=1)
    result = dot_nt(value, weight_ref[...]).astype(BF16)
    for t in range(out_ref.shape[0]):
        out_ref[t] = result


def gate_up(
    parts_ref, residual_ref, gain_ref, gate_ref, up_ref, out_ref, hidden_ref, gate_scr, up_scr, out_scr
):
    requests = residual_ref.shape[0]
    copies, pairs = out_ref.shape[:2]
    blocks = gate_ref.shape[1] // LANES
    hidden = residual_ref[...].astype(F32)
    for t in range(parts_ref.shape[0]):
        hidden = hidden + parts_ref[t].astype(F32)
    hidden_ref[...] = hidden
    squares = jnp.sum(hidden * hidden, axis=1, keepdims=True)
    shape = (requests, LANES)
    diagonal = iota(shape, 0) == iota(shape, 1) % requests
    squares = jnp.sum(jnp.where(diagonal, squares, 0.0), axis=0, keepdims=True)
    high = squares.astype(BF16).astype(F32)
    row = iota((8, LANES), 0)
    squares = jnp.where(row == 0, high, jnp.where(row == 1, squares - high, 0.0))
    gained = (hidden * gain_ref[...].astype(F32)[None, :]).astype(BF16)
    for weight_ref, scr in ((gate_ref, gate_scr), (up_ref, up_scr)):
        part = dot(gained, weight_ref[...])
        for c in range(blocks):
            scr[c * requests : (c + 1) * requests] = part[:, c * LANES : (c + 1) * LANES]
    for k in range(copies):
        start = 2 * k * pairs
        own = slice(k * SHARE, k * SHARE + requests)
        out_scr[start : start + requests] = gate_scr[own]
        out_scr[start + SHARE : start + SHARE + requests] = up_scr[own]
        out_scr[start + 2 * SHARE : start + 2 * SHARE + 8] = squares
    for k in range(copies):
        for i in range(pairs):
            start = 2 * (k * pairs + i)
            out_ref[k, i] = out_scr[start : start + 2].astype(BF16)


def activate(me_ref, parts_ref, out_ref, scr):
    copies, pairs = out_ref.shape[:2]
    requests = REQUESTS
    total = parts_ref[0].astype(F32)
    for k in range(1, copies):
        total = total + parts_ref[k].astype(F32)
    for i in range(parts_ref.shape[1]):
        scr[2 * i : 2 * i + 2] = total[i]
    row = iota((requests, LANES), 0)
    mine = iota(row.shape, 1) == (me_ref[0] * SHARE + row) % requests
    squares = scr[2 * SHARE : 2 * SHARE + 1] + scr[2 * SHARE + 1 : 2 * SHARE + 2]
    squares = jnp.sum(jnp.where(mine, squares, 0.0), axis=1, keepdims=True)
    scale = lax.rsqrt(squares / D + 1e-06)
    gate_sum = scr[:requests] * scale
    up_sum = scr[SHARE : SHARE + requests] * scale
    result = jnp.where(row < SHARE, jax.nn.silu(gate_sum) * up_sum, 0.0)
    for i in range(pairs):
        pair = result[2 * i : 2 * i + 2].astype(BF16)
        for k in range(copies):
            out_ref[k, i] = pair


def project_down(parts_ref, weight_ref, out_ref, scr):
    copies, pairs = parts_ref.shape[:2]
    requests = out_ref.shape[1]
    for k in range(copies):
        for i in range(pairs):
            start = k * SHARE + 2 * i
            scr[start : start + 2] = parts_ref[k, i].astype(F32)
    blocks = weight_ref.shape[1] // LANES
    cols = [scr[c * requests : (c + 1) * requests].astype(BF16) for c in range(blocks)]
    result = dot_nt(jnp.concatenate(cols, axis=1), weight_ref[...]).astype(BF16)
    for t in range(out_ref.shape[0]):
        out_ref[t] = result


def finish(parts_ref, hidden_ref, out_ref):
    total = hidden_ref[...]
    for t in range(parts_ref.shape[0]):
        total = total + parts_ref[t].astype(F32)
    out_ref[...] = total.astype(BF16)


def run(kernel, outs, scratch, *args, smem=0, limit=16):
    shapes = [jax.ShapeDtypeStruct(shape, dtype) for shape, dtype in outs]
    return pl.pallas_call(
        kernel,
        out_shape=shapes if len(shapes) > 1 else shapes[0],
        in_specs=[SMEM] * smem + [VMEM] * (len(args) - smem),
        out_specs=[VMEM] * len(shapes) if len(shapes) > 1 else VMEM,
        scratch_shapes=[pltpu.VMEM(shape, dtype) for shape, dtype in scratch],
        compiler_params=pltpu.CompilerParams(vmem_limit_bytes=limit * 2**20),
    )(*args)


def exchange(x, axis, groups=None):
    return lax.all_to_all(x, axis, 0, 0, axis_index_groups=groups)


def on_device(
    q_nope,
    q_rope,
    w_absorb,
    w_value,
    w_out,
    kv_cache,
    new_latent,
    lengths,
    page_table,
    residual,
    norm_gain,
    w_gate,
    w_up,
    w_down,
):
    requests = q_nope.shape[0]
    heads, nope, latent = w_absorb.shape
    slots, page_len, ctx = kv_cache.shape
    n_kv = lax.axis_size("kv")
    n_tp = lax.axis_size("tp")
    share = heads // CLASSES
    width = residual.shape[1]
    units = w_gate.shape[1]
    scale = 1.0 / math.sqrt(nope + ctx - latent)
    me = lax.axis_index("kv").astype(jnp.int32).reshape(1)

    pages, new = pl.pallas_call(
        functools.partial(attend, scale),
        out_shape=[
            jax.ShapeDtypeStruct((n_kv, slots * share // 2 + 1, 2, LANES), BF16),
            jax.ShapeDtypeStruct((heads, requests, 2 * LANES), F32),
        ],
        in_specs=[SMEM] + [HBM] * 8,
        out_specs=[VMEM] * 2,
        scratch_shapes=[
            pltpu.SMEM((requests,), jnp.int32),
            pltpu.VMEM(page_table.shape, jnp.int32),
            pltpu.VMEM(q_nope.shape, BF16),
            pltpu.VMEM(q_rope.shape, BF16),
            pltpu.VMEM(w_absorb.shape, BF16),
            pltpu.VMEM((slots, ctx, page_len), BF16),
            pltpu.VMEM(w_value.shape, BF16),
            pltpu.VMEM(new_latent.shape, BF16),
            pltpu.VMEM((latent // LANES + 1, heads * slots, LANES), F32),
            pltpu.VMEM((latent // LANES + 2, heads * slots, LANES), F32),
            pltpu.SemaphoreType.DMA((8,)),
        ],
        compiler_params=pltpu.CompilerParams(vmem_limit_bytes=24 * 2**20),
    )(
        me,
        *(
            pltpu.with_memory_space_constraint(x, pltpu.HBM)
            for x in (
                lengths,
                page_table,
                q_nope,
                q_rope,
                w_absorb,
                jnp.swapaxes(kv_cache, 1, 2),
                w_value,
                new_latent,
            )
        ),
    )
    pages = exchange(pages, "kv")
    value = run(
        combine,
        [((CLASSES, requests, share * LANES), BF16)],
        [((share, n_kv * slots, LANES), F32), ((share * n_kv, LANES), F32)],
        me,
        page_table,
        pages,
        new,
        smem=1,
    )
    groups = [list(range(k, k + CLASSES)) for k in range(0, n_kv, CLASSES)]
    value = exchange(value, "kv", groups)
    attention = run(attention_out, [((n_tp, requests, width), BF16)], [], value, w_out.T)
    attention = exchange(attention, "tp")
    rows = units // LANES * requests
    pairs = SHARE + 1
    sums, hidden = run(
        gate_up,
        [((n_kv, pairs, 2, LANES), BF16), ((requests, width), F32)],
        [((rows + requests, LANES), F32)] * 2 + [((2 * n_kv * pairs + 8, LANES), F32)],
        attention,
        residual,
        norm_gain,
        w_gate,
        w_up,
    )
    sums = exchange(sums, "kv")
    activation = run(
        activate,
        [((n_kv, (SHARE + 1) // 2, 2, LANES), BF16)],
        [((2 * SHARE + requests, LANES), F32)],
        me,
        sums,
        smem=1,
    )
    activation = exchange(activation, "kv")
    down = run(
        project_down,
        [((n_tp, requests, width), BF16)],
        [((rows + requests, LANES), F32)],
        activation,
        w_down.T,
    )
    down = exchange(down, "tp")
    return run(finish, [((requests, width), BF16)], [], down, hidden)


def solution(mesh):
    return jax.shard_map(
        on_device,
        mesh=mesh,
        in_specs=(
            P(None, "tp"),
            P(None, "tp"),
            P("tp", None, None),
            P("tp", None, None),
            P("tp", "kv"),
            P("kv", None, None),
            P(),
            P(),
            P(),
            P(None, "kv"),
            P("kv"),
            P("kv", "tp"),
            P("kv", "tp"),
            P("tp", "kv"),
        ),
        out_specs=P(None, "kv"),
        check_vma=False,
    )
```

```python
import functools
import math

import jax
import jax.numpy as jnp
from jax import lax
from jax.experimental import pallas as pl
from jax.experimental.pallas import tpu as pltpu
from jax.sharding import PartitionSpec as P

D = 7168
LOW = -1e30
LANES = 128
CLASSES = 8
REQUESTS = 16
LEAD = 18
LEAD_NEAR = 2
SHARE = 9
STATS = 6
F32 = jnp.float32
BF16 = jnp.bfloat16
HIGHEST = lax.Precision.HIGHEST
VMEM = pl.BlockSpec(memory_space=pltpu.VMEM)
SMEM = pl.BlockSpec(memory_space=pltpu.SMEM)
HBM = pl.BlockSpec(memory_space=pltpu.HBM)


def dot(a, b, precision=None):
    return jnp.dot(a, b, preferred_element_type=F32, precision=precision)


def dot_nt(a, b):
    return lax.dot_general(a, b, (((1,), (1,)), ((), ())), preferred_element_type=F32)


def dot_tn(a, b):
    return lax.dot_general(a, b, (((0,), (0,)), ((), ())), preferred_element_type=F32)


def iota(shape, dim):
    return lax.broadcasted_iota(jnp.int32, shape, dim)


def in_thirds(x):
    high = x.astype(BF16).astype(F32)
    middle = (x - high).astype(BF16).astype(F32)
    low = x - high - middle
    place = iota(x.shape, 1) % 3
    return jnp.where(place == 0, high, jnp.where(place == 1, middle, low))


def attend(
    scale,
    me_ref,
    lengths_hbm,
    table_hbm,
    q_nope_hbm,
    q_rope_hbm,
    absorb_hbm,
    pages_hbm,
    value_hbm,
    new_hbm,
    out_ref,
    new_out_ref,
    lengths_ref,
    table_ref,
    q_nope_ref,
    q_rope_ref,
    absorb_ref,
    pages_ref,
    value_ref,
    new_ref,
    q_scr,
    acc_scr,
    sems,
):
    heads, nope, latent = absorb_ref.shape
    slots, ctx, page_len = pages_ref.shape
    rope = ctx - latent
    requests = new_ref.shape[0]
    me = me_ref[0]
    blocks = latent // LANES

    def fetch(source, target, sem):
        copy = pltpu.make_async_copy(source, target, sem)
        copy.start()
        return copy

    lengths_in = fetch(lengths_hbm, lengths_ref, sems.at[0])
    table_in = fetch(table_hbm, table_ref, sems.at[1])
    q_nope_in = fetch(q_nope_hbm, q_nope_ref, sems.at[2])
    q_rope_in = fetch(q_rope_hbm, q_rope_ref, sems.at[3])
    new_in = fetch(new_hbm, new_ref, sems.at[4])
    absorb_in = fetch(absorb_hbm, absorb_ref, sems.at[5])
    pages_in = fetch(pages_hbm, pages_ref, sems.at[6])
    value_in = fetch(value_hbm, value_ref, sems.at[7])

    lengths_in.wait()
    table_in.wait()
    table = table_ref[...]
    row = iota(table.shape, 0)
    left = iota(table.shape, 1) * -page_len
    for r in range(requests):
        left = left + jnp.where(row == r, lengths_ref[r], 0)
    left = left.astype(F32)
    owner = jnp.zeros((requests, slots), F32)
    tokens = []
    for s in range(slots):
        match = table == me * slots + s
        column = jnp.max(jnp.where(match, 1.0, 0.0), axis=1, keepdims=True)
        owner = owner + jnp.where(iota(owner.shape, 1) == s, column, 0.0)
        found = jnp.sum(jnp.where(match, left, 0.0), axis=1, keepdims=True)
        tokens.append(jnp.sum(found, axis=0, keepdims=True).astype(jnp.int32))
    owner = owner.astype(BF16)

    q_nope_in.wait()
    q_rope_in.wait()
    new_in.wait()
    fresh = new_ref[...].astype(F32)
    fresh_rope = jnp.concatenate([fresh[:, latent:]] * 2, axis=1)
    q_nope = jnp.concatenate(
        [dot_tn(owner, q_nope_ref[...]), q_nope_ref[...].astype(F32)], axis=0
    ).astype(BF16)
    picked_rope = dot_tn(owner, q_rope_ref[...])
    first_half = iota((requests, LANES), 1) < rope
    absorb_in.wait()
    for h in range(heads):
        q_lat = dot(q_nope[:, h * nope : (h + 1) * nope], absorb_ref[h])
        q_lat = q_lat.astype(BF16).astype(F32)
        rows = slice(h * slots, (h + 1) * slots)
        pair = slice(h // 2 * LANES, (h // 2 + 1) * LANES)
        products = q_rope_ref[:, pair].astype(F32) * fresh_rope
        products = jnp.where(first_half == (h % 2 == 0), products, 0.0)
        for c in range(blocks):
            lanes = slice(c * LANES, (c + 1) * LANES)
            q_scr[c, rows] = q_lat[:slots, lanes]
            products = products + q_lat[slots:, lanes] * fresh[:, lanes]
        q_scr[blocks, rows, :rope] = picked_rope[:, h * rope : (h + 1) * rope]
        new_score = jnp.sum(products, axis=1, keepdims=True) * scale
        new_out_ref[h, :, LANES:] = jnp.broadcast_to(new_score, (requests, LANES))
    pages_in.wait()

    all_scores = []
    for s in range(slots):
        every = pl.ds(s, heads, stride=slots)
        q = [q_scr[c, every, :] for c in range(blocks + 1)]
        q = jnp.concatenate(q, axis=1)[:, :ctx].astype(BF16)
        all_scores.append(dot(q, pages_ref[s]))
    all_weights = []
    for s in range(slots):
        live = iota((heads, page_len), 1) < tokens[s]
        scores = jnp.where(live, all_scores[s] * scale, LOW)
        most = jnp.max(scores, axis=1, keepdims=True)
        weights = jnp.where(live, jnp.exp(scores - most), 0.0).astype(BF16)
        total = jnp.sum(weights.astype(F32), axis=1, keepdims=True)
        rows = slice(s * heads, (s + 1) * heads)
        acc_scr[blocks, rows] = jnp.broadcast_to(most, (heads, LANES))
        acc_scr[blocks + 1, rows] = jnp.broadcast_to(total, (heads, LANES))
        all_weights.append(weights)
    for s in range(slots):
        rows = slice(s * heads, (s + 1) * heads)
        acc = dot_nt(all_weights[s], pages_ref[s, :latent, :])
        for c in range(blocks):
            acc_scr[c, rows] = acc[:, c * LANES : (c + 1) * LANES]

    value_in.wait()
    all_valued = []
    for h in range(heads):
        every = pl.ds(h, slots, stride=heads)
        acc = jnp.concatenate([acc_scr[c, every, :] for c in range(blocks)], axis=1)
        high = acc.astype(BF16).astype(F32)
        rows = jnp.concatenate([high, acc - high, fresh[:, :latent]], axis=0).astype(BF16)
        all_valued.append(dot(rows, value_ref[h]))
    for h in range(heads):
        new_out_ref[h, :, :LANES] = all_valued[h][2 * slots :]
    copies, pairs = out_ref.shape[:2]
    share = heads // CLASSES
    row = iota((slots, LANES), 0)
    lane = iota((slots, LANES), 1)
    for part in range(CLASSES):
        stats = jnp.zeros((slots, LANES), F32)
        rows = []
        for i in range(share):
            h = part * share + i
            every = pl.ds(h, slots, stride=heads)
            stat = jnp.where(
                lane % STATS < 3, acc_scr[blocks, every, :], acc_scr[blocks + 1, every, :]
            )
            stat = jnp.where(lane // STATS == row, stat, 0.0)
            stats = jnp.where(row == i, jnp.sum(stat, axis=0, keepdims=True), stats)
            rows.append(all_valued[h][:slots] + all_valued[h][slots : 2 * slots])
        rows = jnp.concatenate(rows + [in_thirds(stats)], axis=0)
        for i in range(pairs):
            pair = rows[2 * i : 2 * i + 2].astype(BF16)
            for k in range(part, copies, CLASSES):
                out_ref[(k - LEAD) % copies, i] = pair


def combine(me_ref, table_ref, parts_ref, new_ref, out_ref, acc_scr, stat_scr):
    sources, pairs = parts_ref.shape[:2]
    heads, requests, _ = new_ref.shape
    share = heads // CLASSES
    slots = acc_scr.shape[1]
    slots_each = slots // sources
    first = me_ref[0] % CLASSES * share
    for k in range(sources):
        for i in range(pairs - 1):
            start = k * slots_each + 2 * i % slots_each
            pair = parts_ref[(k - LEAD) % sources, i].astype(F32)
            acc_scr[2 * i // slots_each, start : start + 2] = pair
        pair = parts_ref[(k - LEAD) % sources, pairs - 1].astype(F32)
        stat_scr[2 * k : 2 * k + 2] = pair

    stats = stat_scr[...].astype(BF16)
    place = iota((LANES, slots), 0)
    here = place // STATS == iota((LANES, slots), 1) % slots_each
    top_lanes = jnp.where(here & (place % STATS < 3), 1.0, 0.0).astype(BF16)
    sum_lanes = jnp.where(here & (place % STATS >= 3), 1.0, 0.0).astype(BF16)
    top_rows = dot(stats, top_lanes)
    sum_rows = dot(stats, sum_lanes)
    row = iota(top_rows.shape, 0)
    source = iota(top_rows.shape, 1) // slots_each

    table = table_ref[...]
    slot = iota((requests, slots), 1)
    owns = slot < 0
    for j in range(table.shape[1]):
        owns = owns | (table[:, j : j + 1] == slot)

    factors, keeps, totals = [], [], []
    for i in range(share):
        mine = row == 2 * source + i
        page_max = jnp.sum(jnp.where(mine, top_rows, 0.0), axis=0, keepdims=True)
        page_sum = jnp.sum(jnp.where(mine, sum_rows, 0.0), axis=0, keepdims=True)
        page_max = jnp.where(owns, page_max, LOW)
        new_score = new_ref[first + i, :, LANES:]
        top = jnp.maximum(jnp.max(page_max, axis=1, keepdims=True), new_score)
        factor = jnp.where(owns, jnp.exp(page_max - top[:, :1]), 0.0)
        totals.append(jnp.sum(factor * page_sum, axis=1, keepdims=True))
        high = factor.astype(BF16).astype(F32)
        factors.append(jnp.concatenate([high, factor - high], axis=0).astype(BF16))
        keeps.append(jnp.exp(new_score - top))
    sums = [dot(factors[i], acc_scr[i].astype(BF16)) for i in range(share)]
    values = []
    for i in range(share):
        both = sums[i][:requests] + sums[i][requests:]
        value = both + keeps[i] * new_ref[first + i, :, :LANES]
        values.append((value / (totals[i] + keeps[i])).astype(BF16))
    values = jnp.concatenate(values, axis=1)
    for k in range(CLASSES):
        out_ref[k] = values


def attention_out(parts_ref, weight_ref, out_ref):
    parts = [parts_ref[(k - LEAD_NEAR) % CLASSES] for k in range(CLASSES)]
    value = jnp.concatenate(parts, axis=1)
    result = dot_nt(value, weight_ref[...]).astype(BF16)
    for t in range(out_ref.shape[0]):
        out_ref[t] = result


def gate_up(
    parts_ref, residual_ref, gain_ref, gate_ref, up_ref, out_ref, hidden_ref, gate_scr, up_scr, out_scr
):
    requests = residual_ref.shape[0]
    copies, pairs = out_ref.shape[:2]
    blocks = gate_ref.shape[1] // LANES
    hidden = residual_ref[...].astype(F32)
    for t in range(parts_ref.shape[0]):
        hidden = hidden + parts_ref[t].astype(F32)
    hidden_ref[...] = hidden
    squares = jnp.sum(hidden * hidden, axis=1, keepdims=True)
    shape = (requests, LANES)
    diagonal = iota(shape, 0) == iota(shape, 1) % requests
    squares = jnp.sum(jnp.where(diagonal, squares, 0.0), axis=0, keepdims=True)
    high = squares.astype(BF16).astype(F32)
    row = iota((8, LANES), 0)
    squares = jnp.where(row == 0, high, jnp.where(row == 1, squares - high, 0.0))
    gained = (hidden * gain_ref[...].astype(F32)[None, :]).astype(BF16)
    for weight_ref, scr in ((gate_ref, gate_scr), (up_ref, up_scr)):
        part = dot(gained, weight_ref[...])
        for c in range(blocks):
            scr[c * requests : (c + 1) * requests] = part[:, c * LANES : (c + 1) * LANES]
    for k in range(copies):
        start = 2 * k * pairs
        own = slice(k * SHARE, k * SHARE + requests)
        out_scr[start : start + requests] = gate_scr[own]
        out_scr[start + SHARE : start + SHARE + requests] = up_scr[own]
        out_scr[start + 2 * SHARE : start + 2 * SHARE + 8] = squares
    for k in range(copies):
        for i in range(pairs):
            start = 2 * (k * pairs + i)
            out_ref[(k - LEAD) % copies, i] = out_scr[start : start + 2].astype(BF16)


def activate(me_ref, parts_ref, out_ref, scr):
    copies, pairs = out_ref.shape[:2]
    requests = REQUESTS
    total = parts_ref[0].astype(F32)
    for k in range(1, copies):
        total = total + parts_ref[k].astype(F32)
    for i in range(parts_ref.shape[1]):
        scr[2 * i : 2 * i + 2] = total[i]
    row = iota((requests, LANES), 0)
    mine = iota(row.shape, 1) == (me_ref[0] * SHARE + row) % requests
    squares = scr[2 * SHARE : 2 * SHARE + 1] + scr[2 * SHARE + 1 : 2 * SHARE + 2]
    squares = jnp.sum(jnp.where(mine, squares, 0.0), axis=1, keepdims=True)
    scale = lax.rsqrt(squares / D + 1e-06)
    gate_sum = scr[:requests] * scale
    up_sum = scr[SHARE : SHARE + requests] * scale
    result = jnp.where(row < SHARE, jax.nn.silu(gate_sum) * up_sum, 0.0)
    for i in range(pairs):
        pair = result[2 * i : 2 * i + 2].astype(BF16)
        for k in range(copies):
            out_ref[k, i] = pair


def project_down(parts_ref, weight_ref, out_ref, scr):
    copies, pairs = parts_ref.shape[:2]
    requests = out_ref.shape[1]
    for k in range(copies):
        for i in range(pairs):
            start = k * SHARE + 2 * i
            scr[start : start + 2] = parts_ref[(k - LEAD) % copies, i].astype(F32)
    blocks = weight_ref.shape[1] // LANES
    cols = [scr[c * requests : (c + 1) * requests].astype(BF16) for c in range(blocks)]
    result = dot_nt(jnp.concatenate(cols, axis=1), weight_ref[...]).astype(BF16)
    for t in range(out_ref.shape[0]):
        out_ref[t] = result


def finish(parts_ref, hidden_ref, out_ref):
    total = hidden_ref[...]
    for t in range(parts_ref.shape[0]):
        total = total + parts_ref[t].astype(F32)
    out_ref[...] = total.astype(BF16)


def run(kernel, outs, scratch, *args, smem=0, limit=16):
    shapes = [jax.ShapeDtypeStruct(shape, dtype) for shape, dtype in outs]
    return pl.pallas_call(
        kernel,
        out_shape=shapes if len(shapes) > 1 else shapes[0],
        in_specs=[SMEM] * smem + [VMEM] * (len(args) - smem),
        out_specs=[VMEM] * len(shapes) if len(shapes) > 1 else VMEM,
        scratch_shapes=[pltpu.VMEM(shape, dtype) for shape, dtype in scratch],
        compiler_params=pltpu.CompilerParams(vmem_limit_bytes=limit * 2**20),
    )(*args)


def exchange(x, axis, groups=None):
    return lax.all_to_all(x, axis, 0, 0, axis_index_groups=groups)


def on_device(
    q_nope,
    q_rope,
    w_absorb,
    w_value,
    w_out,
    kv_cache,
    new_latent,
    lengths,
    page_table,
    residual,
    norm_gain,
    w_gate,
    w_up,
    w_down,
):
    requests = q_nope.shape[0]
    heads, nope, latent = w_absorb.shape
    slots, page_len, ctx = kv_cache.shape
    n_kv = lax.axis_size("kv")
    n_tp = lax.axis_size("tp")
    share = heads // CLASSES
    width = residual.shape[1]
    units = w_gate.shape[1]
    scale = 1.0 / math.sqrt(nope + ctx - latent)
    me = lax.axis_index("kv").astype(jnp.int32).reshape(1)

    pages, new = pl.pallas_call(
        functools.partial(attend, scale),
        out_shape=[
            jax.ShapeDtypeStruct((n_kv, slots * share // 2 + 1, 2, LANES), BF16),
            jax.ShapeDtypeStruct((heads, requests, 2 * LANES), F32),
        ],
        in_specs=[SMEM] + [HBM] * 8,
        out_specs=[VMEM] * 2,
        scratch_shapes=[
            pltpu.SMEM((requests,), jnp.int32),
            pltpu.VMEM(page_table.shape, jnp.int32),
            pltpu.VMEM(q_nope.shape, BF16),
            pltpu.VMEM(q_rope.shape, BF16),
            pltpu.VMEM(w_absorb.shape, BF16),
            pltpu.VMEM((slots, ctx, page_len), BF16),
            pltpu.VMEM(w_value.shape, BF16),
            pltpu.VMEM(new_latent.shape, BF16),
            pltpu.VMEM((latent // LANES + 1, heads * slots, LANES), F32),
            pltpu.VMEM((latent // LANES + 2, heads * slots, LANES), F32),
            pltpu.SemaphoreType.DMA((8,)),
        ],
        compiler_params=pltpu.CompilerParams(vmem_limit_bytes=24 * 2**20),
    )(
        me,
        *(
            pltpu.with_memory_space_constraint(x, pltpu.HBM)
            for x in (
                lengths,
                page_table,
                q_nope,
                q_rope,
                w_absorb,
                jnp.swapaxes(kv_cache, 1, 2),
                w_value,
                new_latent,
            )
        ),
    )
    everyone = [[(LEAD + k) % n_kv for k in range(n_kv)]]
    pages = exchange(pages, "kv", everyone)
    value = run(
        combine,
        [((CLASSES, requests, share * LANES), BF16)],
        [((share, n_kv * slots, LANES), F32), ((share * n_kv, LANES), F32)],
        me,
        page_table,
        pages,
        new,
        smem=1,
    )
    groups = [
        [first + (LEAD_NEAR + k) % CLASSES for k in range(CLASSES)]
        for first in range(0, n_kv, CLASSES)
    ]
    value = exchange(value, "kv", groups)
    attention = run(attention_out, [((n_tp, requests, width), BF16)], [], value, w_out.T)
    attention = exchange(attention, "tp", [[4, 5, 2, 3, 6, 7, 0, 1]])
    rows = units // LANES * requests
    pairs = SHARE + 1
    sums, hidden = run(
        gate_up,
        [((n_kv, pairs, 2, LANES), BF16), ((requests, width), F32)],
        [((rows + requests, LANES), F32)] * 2 + [((2 * n_kv * pairs + 8, LANES), F32)],
        attention,
        residual,
        norm_gain,
        w_gate,
        w_up,
    )
    sums = exchange(sums, "kv", everyone)
    activation = run(
        activate,
        [((n_kv, (SHARE + 1) // 2, 2, LANES), BF16)],
        [((2 * SHARE + requests, LANES), F32)],
        me,
        sums,
        smem=1,
    )
    activation = exchange(activation, "kv", everyone)
    down = run(
        project_down,
        [((n_tp, requests, width), BF16)],
        [((rows + requests, LANES), F32)],
        activation,
        w_down.T,
    )
    down = exchange(down, "tp", [[4, 5, 2, 3, 6, 7, 0, 1]])
    return run(finish, [((requests, width), BF16)], [], down, hidden)


def solution(mesh):
    return jax.shard_map(
        on_device,
        mesh=mesh,
        in_specs=(
            P(None, "tp"),
            P(None, "tp"),
            P("tp", None, None),
            P("tp", None, None),
            P("tp", "kv"),
            P("kv", None, None),
            P(),
            P(),
            P(),
            P(None, "kv"),
            P("kv"),
            P("kv", "tp"),
            P("kv", "tp"),
            P("tp", "kv"),
        ),
        out_specs=P(None, "kv"),
        check_vma=False,
    )
```

```python
import functools
import math

import jax
import jax.numpy as jnp
from jax import lax
from jax.experimental import pallas as pl
from jax.experimental.pallas import tpu as pltpu
from jax.sharding import PartitionSpec as P

D = 7168
LOW = -1e30
LANES = 128
CLASSES = 8
REQUESTS = 16
LEAD = 23
LEAD_NEAR = 2
SHARE = 9
STATS = 6
F32 = jnp.float32
BF16 = jnp.bfloat16
HIGHEST = lax.Precision.HIGHEST
VMEM = pl.BlockSpec(memory_space=pltpu.VMEM)
SMEM = pl.BlockSpec(memory_space=pltpu.SMEM)
HBM = pl.BlockSpec(memory_space=pltpu.HBM)


def dot(a, b, precision=None):
    return jnp.dot(a, b, preferred_element_type=F32, precision=precision)


def dot_nt(a, b):
    return lax.dot_general(a, b, (((1,), (1,)), ((), ())), preferred_element_type=F32)


def dot_tn(a, b):
    return lax.dot_general(a, b, (((0,), (0,)), ((), ())), preferred_element_type=F32)


def iota(shape, dim):
    return lax.broadcasted_iota(jnp.int32, shape, dim)


def in_thirds(x):
    high = x.astype(BF16).astype(F32)
    middle = (x - high).astype(BF16).astype(F32)
    low = x - high - middle
    place = iota(x.shape, 1) % 3
    return jnp.where(place == 0, high, jnp.where(place == 1, middle, low))


def attend(
    scale,
    me_ref,
    lengths_hbm,
    table_hbm,
    q_nope_hbm,
    q_rope_hbm,
    absorb_hbm,
    pages_hbm,
    value_hbm,
    new_hbm,
    out_ref,
    new_out_ref,
    lengths_ref,
    table_ref,
    q_nope_ref,
    q_rope_ref,
    absorb_ref,
    pages_ref,
    value_ref,
    new_ref,
    q_scr,
    acc_scr,
    sems,
):
    heads, nope, latent = absorb_ref.shape
    slots, ctx, page_len = pages_ref.shape
    rope = ctx - latent
    requests = new_ref.shape[0]
    me = me_ref[0]
    blocks = latent // LANES

    def fetch(source, target, sem):
        copy = pltpu.make_async_copy(source, target, sem)
        copy.start()
        return copy

    lengths_in = fetch(lengths_hbm, lengths_ref, sems.at[0])
    table_in = fetch(table_hbm, table_ref, sems.at[1])
    q_nope_in = fetch(q_nope_hbm, q_nope_ref, sems.at[2])
    q_rope_in = fetch(q_rope_hbm, q_rope_ref, sems.at[3])
    new_in = fetch(new_hbm, new_ref, sems.at[4])
    absorb_in = fetch(absorb_hbm, absorb_ref, sems.at[5])
    pages_in = fetch(pages_hbm, pages_ref, sems.at[6])
    value_in = fetch(value_hbm, value_ref, sems.at[7])

    lengths_in.wait()
    table_in.wait()
    table = table_ref[...]
    row = iota(table.shape, 0)
    left = iota(table.shape, 1) * -page_len
    for r in range(requests):
        left = left + jnp.where(row == r, lengths_ref[r], 0)
    left = left.astype(F32)
    owner = jnp.zeros((requests, slots), F32)
    tokens = []
    for s in range(slots):
        match = table == me * slots + s
        column = jnp.max(jnp.where(match, 1.0, 0.0), axis=1, keepdims=True)
        owner = owner + jnp.where(iota(owner.shape, 1) == s, column, 0.0)
        found = jnp.sum(jnp.where(match, left, 0.0), axis=1, keepdims=True)
        tokens.append(jnp.sum(found, axis=0, keepdims=True).astype(jnp.int32))
    owner = owner.astype(BF16)

    q_nope_in.wait()
    q_rope_in.wait()
    new_in.wait()
    fresh = new_ref[...].astype(F32)
    fresh_rope = jnp.concatenate([fresh[:, latent:]] * 2, axis=1)
    q_nope = jnp.concatenate(
        [dot_tn(owner, q_nope_ref[...]), q_nope_ref[...].astype(F32)], axis=0
    ).astype(BF16)
    picked_rope = dot_tn(owner, q_rope_ref[...])
    first_half = iota((requests, LANES), 1) < rope
    absorb_in.wait()
    for h in range(heads):
        q_lat = dot(q_nope[:, h * nope : (h + 1) * nope], absorb_ref[h])
        q_lat = q_lat.astype(BF16).astype(F32)
        rows = slice(h * slots, (h + 1) * slots)
        pair = slice(h // 2 * LANES, (h // 2 + 1) * LANES)
        products = q_rope_ref[:, pair].astype(F32) * fresh_rope
        products = jnp.where(first_half == (h % 2 == 0), products, 0.0)
        for c in range(blocks):
            lanes = slice(c * LANES, (c + 1) * LANES)
            q_scr[c, rows] = q_lat[:slots, lanes]
            products = products + q_lat[slots:, lanes] * fresh[:, lanes]
        q_scr[blocks, rows, :rope] = picked_rope[:, h * rope : (h + 1) * rope]
        new_score = jnp.sum(products, axis=1, keepdims=True) * scale
        new_out_ref[h, :, LANES:] = jnp.broadcast_to(new_score, (requests, LANES))
    pages_in.wait()

    all_scores = []
    for s in range(slots):
        every = pl.ds(s, heads, stride=slots)
        q = [q_scr[c, every, :] for c in range(blocks + 1)]
        q = jnp.concatenate(q, axis=1)[:, :ctx].astype(BF16)
        all_scores.append(dot(q, pages_ref[s]))
    all_weights = []
    for s in range(slots):
        live = iota((heads, page_len), 1) < tokens[s]
        scores = jnp.where(live, all_scores[s] * scale, LOW)
        most = jnp.max(scores, axis=1, keepdims=True)
        weights = jnp.where(live, jnp.exp(scores - most), 0.0).astype(BF16)
        total = jnp.sum(weights.astype(F32), axis=1, keepdims=True)
        rows = slice(s * heads, (s + 1) * heads)
        acc_scr[blocks, rows] = jnp.broadcast_to(most, (heads, LANES))
        acc_scr[blocks + 1, rows] = jnp.broadcast_to(total, (heads, LANES))
        all_weights.append(weights)
    for s in range(slots):
        rows = slice(s * heads, (s + 1) * heads)
        acc = dot_nt(all_weights[s], pages_ref[s, :latent, :])
        for c in range(blocks):
            acc_scr[c, rows] = acc[:, c * LANES : (c + 1) * LANES]

    value_in.wait()
    all_valued = []
    for h in range(heads):
        every = pl.ds(h, slots, stride=heads)
        acc = jnp.concatenate([acc_scr[c, every, :] for c in range(blocks)], axis=1)
        high = acc.astype(BF16).astype(F32)
        rows = jnp.concatenate([high, acc - high, fresh[:, :latent]], axis=0).astype(BF16)
        all_valued.append(dot(rows, value_ref[h]))
    for h in range(heads):
        new_out_ref[h, :, :LANES] = all_valued[h][2 * slots :]
    copies, pairs = out_ref.shape[:2]
    share = heads // CLASSES
    row = iota((slots, LANES), 0)
    lane = iota((slots, LANES), 1)
    for part in range(CLASSES):
        stats = jnp.zeros((slots, LANES), F32)
        rows = []
        for i in range(share):
            h = part * share + i
            every = pl.ds(h, slots, stride=heads)
            stat = jnp.where(
                lane % STATS < 3, acc_scr[blocks, every, :], acc_scr[blocks + 1, every, :]
            )
            stat = jnp.where(lane // STATS == row, stat, 0.0)
            stats = jnp.where(row == i, jnp.sum(stat, axis=0, keepdims=True), stats)
            rows.append(all_valued[h][:slots] + all_valued[h][slots : 2 * slots])
        rows = jnp.concatenate(rows + [in_thirds(stats)], axis=0)
        for i in range(pairs):
            pair = rows[2 * i : 2 * i + 2].astype(BF16)
            for k in range(part, copies, CLASSES):
                out_ref[(k - LEAD) % copies, i] = pair


def combine(me_ref, table_ref, parts_ref, new_ref, out_ref, acc_scr, stat_scr):
    sources, pairs = parts_ref.shape[:2]
    heads, requests, _ = new_ref.shape
    share = heads // CLASSES
    slots = acc_scr.shape[1]
    slots_each = slots // sources
    first = me_ref[0] % CLASSES * share
    for k in range(sources):
        for i in range(pairs - 1):
            start = k * slots_each + 2 * i % slots_each
            pair = parts_ref[(k - LEAD) % sources, i].astype(F32)
            acc_scr[2 * i // slots_each, start : start + 2] = pair
        pair = parts_ref[(k - LEAD) % sources, pairs - 1].astype(F32)
        stat_scr[2 * k : 2 * k + 2] = pair

    stats = stat_scr[...].astype(BF16)
    place = iota((LANES, slots), 0)
    here = place // STATS == iota((LANES, slots), 1) % slots_each
    top_lanes = jnp.where(here & (place % STATS < 3), 1.0, 0.0).astype(BF16)
    sum_lanes = jnp.where(here & (place % STATS >= 3), 1.0, 0.0).astype(BF16)
    top_rows = dot(stats, top_lanes)
    sum_rows = dot(stats, sum_lanes)
    row = iota(top_rows.shape, 0)
    source = iota(top_rows.shape, 1) // slots_each

    table = table_ref[...]
    slot = iota((requests, slots), 1)
    owns = slot < 0
    for j in range(table.shape[1]):
        owns = owns | (table[:, j : j + 1] == slot)

    factors, keeps, totals = [], [], []
    for i in range(share):
        mine = row == 2 * source + i
        page_max = jnp.sum(jnp.where(mine, top_rows, 0.0), axis=0, keepdims=True)
        page_sum = jnp.sum(jnp.where(mine, sum_rows, 0.0), axis=0, keepdims=True)
        page_max = jnp.where(owns, page_max, LOW)
        new_score = new_ref[first + i, :, LANES:]
        top = jnp.maximum(jnp.max(page_max, axis=1, keepdims=True), new_score)
        factor = jnp.where(owns, jnp.exp(page_max - top[:, :1]), 0.0)
        totals.append(jnp.sum(factor * page_sum, axis=1, keepdims=True))
        high = factor.astype(BF16).astype(F32)
        factors.append(jnp.concatenate([high, factor - high], axis=0).astype(BF16))
        keeps.append(jnp.exp(new_score - top))
    sums = [dot(factors[i], acc_scr[i].astype(BF16)) for i in range(share)]
    values = []
    for i in range(share):
        both = sums[i][:requests] + sums[i][requests:]
        value = both + keeps[i] * new_ref[first + i, :, :LANES]
        values.append((value / (totals[i] + keeps[i])).astype(BF16))
    values = jnp.concatenate(values, axis=1)
    for k in range(CLASSES):
        out_ref[k] = values


def attention_out(parts_ref, weight_ref, out_ref):
    parts = [parts_ref[(k - LEAD_NEAR) % CLASSES] for k in range(CLASSES)]
    value = jnp.concatenate(parts, axis=1)
    result = dot_nt(value, weight_ref[...]).astype(BF16)
    for t in range(out_ref.shape[0]):
        out_ref[t] = result


def gate_up(
    parts_ref, residual_ref, gain_ref, gate_ref, up_ref, out_ref, hidden_ref, gate_scr, up_scr, out_scr
):
    requests = residual_ref.shape[0]
    copies, pairs = out_ref.shape[:2]
    blocks = gate_ref.shape[1] // LANES
    hidden = residual_ref[...].astype(F32)
    for t in range(parts_ref.shape[0]):
        hidden = hidden + parts_ref[t].astype(F32)
    hidden_ref[...] = hidden
    squares = jnp.sum(hidden * hidden, axis=1, keepdims=True)
    shape = (requests, LANES)
    diagonal = iota(shape, 0) == iota(shape, 1) % requests
    squares = jnp.sum(jnp.where(diagonal, squares, 0.0), axis=0, keepdims=True)
    high = squares.astype(BF16).astype(F32)
    row = iota((8, LANES), 0)
    squares = jnp.where(row == 0, high, jnp.where(row == 1, squares - high, 0.0))
    gained = (hidden * gain_ref[...].astype(F32)[None, :]).astype(BF16)
    for weight_ref, scr in ((gate_ref, gate_scr), (up_ref, up_scr)):
        part = dot(gained, weight_ref[...])
        for c in range(blocks):
            scr[c * requests : (c + 1) * requests] = part[:, c * LANES : (c + 1) * LANES]
    for k in range(copies):
        start = 2 * k * pairs
        own = slice(k * SHARE, k * SHARE + requests)
        out_scr[start : start + requests] = gate_scr[own]
        out_scr[start + SHARE : start + SHARE + requests] = up_scr[own]
        out_scr[start + 2 * SHARE : start + 2 * SHARE + 8] = squares
    for k in range(copies):
        for i in range(pairs):
            start = 2 * (k * pairs + i)
            out_ref[(k - LEAD) % copies, i] = out_scr[start : start + 2].astype(BF16)


def activate(me_ref, parts_ref, out_ref, scr):
    copies, pairs = out_ref.shape[:2]
    requests = REQUESTS
    total = parts_ref[0].astype(F32)
    for k in range(1, copies):
        total = total + parts_ref[k].astype(F32)
    for i in range(parts_ref.shape[1]):
        scr[2 * i : 2 * i + 2] = total[i]
    row = iota((requests, LANES), 0)
    mine = iota(row.shape, 1) == (me_ref[0] * SHARE + row) % requests
    squares = scr[2 * SHARE : 2 * SHARE + 1] + scr[2 * SHARE + 1 : 2 * SHARE + 2]
    squares = jnp.sum(jnp.where(mine, squares, 0.0), axis=1, keepdims=True)
    scale = lax.rsqrt(squares / D + 1e-06)
    gate_sum = scr[:requests] * scale
    up_sum = scr[SHARE : SHARE + requests] * scale
    result = jnp.where(row < SHARE, jax.nn.silu(gate_sum) * up_sum, 0.0)
    for i in range(pairs):
        pair = result[2 * i : 2 * i + 2].astype(BF16)
        for k in range(copies):
            out_ref[k, i] = pair


def project_down(parts_ref, weight_ref, out_ref, scr):
    copies, pairs = parts_ref.shape[:2]
    requests = out_ref.shape[1]
    for k in range(copies):
        for i in range(pairs):
            start = k * SHARE + 2 * i
            scr[start : start + 2] = parts_ref[(k - LEAD) % copies, i].astype(F32)
    blocks = weight_ref.shape[1] // LANES
    cols = [scr[c * requests : (c + 1) * requests].astype(BF16) for c in range(blocks)]
    result = dot_nt(jnp.concatenate(cols, axis=1), weight_ref[...]).astype(BF16)
    for t in range(out_ref.shape[0]):
        out_ref[t] = result


def finish(parts_ref, hidden_ref, out_ref):
    total = hidden_ref[...]
    for t in range(parts_ref.shape[0]):
        total = total + parts_ref[t].astype(F32)
    out_ref[...] = total.astype(BF16)


def run(kernel, outs, scratch, *args, smem=0, limit=16):
    shapes = [jax.ShapeDtypeStruct(shape, dtype) for shape, dtype in outs]
    return pl.pallas_call(
        kernel,
        out_shape=shapes if len(shapes) > 1 else shapes[0],
        in_specs=[SMEM] * smem + [VMEM] * (len(args) - smem),
        out_specs=[VMEM] * len(shapes) if len(shapes) > 1 else VMEM,
        scratch_shapes=[pltpu.VMEM(shape, dtype) for shape, dtype in scratch],
        compiler_params=pltpu.CompilerParams(vmem_limit_bytes=limit * 2**20),
    )(*args)


def exchange(x, axis, groups=None):
    return lax.all_to_all(x, axis, 0, 0, axis_index_groups=groups)


def on_device(
    q_nope,
    q_rope,
    w_absorb,
    w_value,
    w_out,
    kv_cache,
    new_latent,
    lengths,
    page_table,
    residual,
    norm_gain,
    w_gate,
    w_up,
    w_down,
):
    requests = q_nope.shape[0]
    heads, nope, latent = w_absorb.shape
    slots, page_len, ctx = kv_cache.shape
    n_kv = lax.axis_size("kv")
    n_tp = lax.axis_size("tp")
    share = heads // CLASSES
    width = residual.shape[1]
    units = w_gate.shape[1]
    scale = 1.0 / math.sqrt(nope + ctx - latent)
    me = lax.axis_index("kv").astype(jnp.int32).reshape(1)

    pages, new = pl.pallas_call(
        functools.partial(attend, scale),
        out_shape=[
            jax.ShapeDtypeStruct((n_kv, slots * share // 2 + 1, 2, LANES), BF16),
            jax.ShapeDtypeStruct((heads, requests, 2 * LANES), F32),
        ],
        in_specs=[SMEM] + [HBM] * 8,
        out_specs=[VMEM] * 2,
        scratch_shapes=[
            pltpu.SMEM((requests,), jnp.int32),
            pltpu.VMEM(page_table.shape, jnp.int32),
            pltpu.VMEM(q_nope.shape, BF16),
            pltpu.VMEM(q_rope.shape, BF16),
            pltpu.VMEM(w_absorb.shape, BF16),
            pltpu.VMEM((slots, ctx, page_len), BF16),
            pltpu.VMEM(w_value.shape, BF16),
            pltpu.VMEM(new_latent.shape, BF16),
            pltpu.VMEM((latent // LANES + 1, heads * slots, LANES), F32),
            pltpu.VMEM((latent // LANES + 2, heads * slots, LANES), F32),
            pltpu.SemaphoreType.DMA((8,)),
        ],
        compiler_params=pltpu.CompilerParams(vmem_limit_bytes=24 * 2**20),
    )(
        me,
        *(
            pltpu.with_memory_space_constraint(x, pltpu.HBM)
            for x in (
                lengths,
                page_table,
                q_nope,
                q_rope,
                w_absorb,
                jnp.swapaxes(kv_cache, 1, 2),
                w_value,
                new_latent,
            )
        ),
    )
    everyone = [[(LEAD + k) % n_kv for k in range(n_kv)]]
    pages = exchange(pages, "kv", everyone)
    value = run(
        combine,
        [((CLASSES, requests, share * LANES), BF16)],
        [((share, n_kv * slots, LANES), F32), ((share * n_kv, LANES), F32)],
        me,
        page_table,
        pages,
        new,
        smem=1,
    )
    groups = [
        [first + (LEAD_NEAR + k) % CLASSES for k in range(CLASSES)]
        for first in range(0, n_kv, CLASSES)
    ]
    value = exchange(value, "kv", groups)
    attention = run(attention_out, [((n_tp, requests, width), BF16)], [], value, w_out.T)
    attention = exchange(attention, "tp", [[4, 5, 2, 3, 6, 7, 0, 1]])
    rows = units // LANES * requests
    pairs = SHARE + 1
    sums, hidden = run(
        gate_up,
        [((n_kv, pairs, 2, LANES), BF16), ((requests, width), F32)],
        [((rows + requests, LANES), F32)] * 2 + [((2 * n_kv * pairs + 8, LANES), F32)],
        attention,
        residual,
        norm_gain,
        w_gate,
        w_up,
    )
    sums = exchange(sums, "kv", everyone)
    activation = run(
        activate,
        [((n_kv, (SHARE + 1) // 2, 2, LANES), BF16)],
        [((2 * SHARE + requests, LANES), F32)],
        me,
        sums,
        smem=1,
    )
    activation = exchange(activation, "kv", everyone)
    down = run(
        project_down,
        [((n_tp, requests, width), BF16)],
        [((rows + requests, LANES), F32)],
        activation,
        w_down.T,
    )
    down = exchange(down, "tp", [[4, 5, 2, 3, 6, 7, 0, 1]])
    return run(finish, [((requests, width), BF16)], [], down, hidden)


def solution(mesh):
    return jax.shard_map(
        on_device,
        mesh=mesh,
        in_specs=(
            P(None, "tp"),
            P(None, "tp"),
            P("tp", None, None),
            P("tp", None, None),
            P("tp", "kv"),
            P("kv", None, None),
            P(),
            P(),
            P(),
            P(None, "kv"),
            P("kv"),
            P("kv", "tp"),
            P("kv", "tp"),
            P("tp", "kv"),
        ),
        out_specs=P(None, "kv"),
        check_vma=False,
    )
```
